512 devices in a mesh: row: 16 (over y, core), col: 32 (over x, z).
Axes of the slice: x: 4, y: 8, z: 8, core: 2. Of those that a mesh axis runs over, the one named last changes fastest.
Arguments:
- w_cycle: bfloat16 [1536, 24576], P('row', 'col'), may hold values from -0.109375 to 0.109375
- amplitudes: bfloat16 [192, 192, 128, 128], P('col', None, 'row'), may hold values from -6 to 6
- occ_count: int32 [8], replicated, may hold values from 1 to 24, 120 in all
- virt_count: int32 [8], replicated, may hold values from 1 to 128, 680 in all
- target: int32 [1], replicated, may hold values from 0 to 7
Outputs:
- cycle: bfloat16 [1536, 24576], P('col', 'row')
The draws below stay inside these ranges and needn't reach their ends.
Inputs may be any that keep to these rules, and one draw needn't show every extreme that they name: `occ_count`: in stored slot order; they sum to 120, and some irrep has exactly 24. `virt_count`: in stored slot order; they sum to 680, and some irrep has exactly 128.
All inputs are finite; a program needn't handle non-finite values.
Results may differ from the reference program's by a relative error of at most 0.019.
Values may be sent and summed in bfloat16 or wider, within the bound.
No kernel may reach another device: no remote copies, remote signals or barrier semaphores. Data moves between devices by JAX's collectives and lax.ppermute only.
A program may use at most 64 MiB of HBM per device.

```python
import math
import jax
import jax.numpy as jnp
import numpy as np
from jax import lax

O = 120
V = 680
IRREPS = 8
OCAP = 24
VCAP = 128
IW = 12
KO = 192
KC = 24576
IA = 1536
KSLICE = 6


def strengthened(result, own_key, source, target, blocks, factor):
    def block_of(axis_at):
        return (jnp.arange(result.shape[axis_at]) // (result.shape[axis_at] // blocks)).reshape((-1,) + (1,) * (result.ndim - 1 - axis_at))

    one_side = jax.random.permutation(own_key, blocks)[block_of(target)]
    far = (block_of(target) + blocks // 2) % blocks
    return jnp.where((block_of(source) == one_side) | (block_of(source) == far), factor * result, result)


def levels(rng, extent, cuts, low, largest):
    def one(axis_at, blocks):
        heights = jax.random.uniform(jax.random.fold_in(jax.random.fold_in(rng, 6), axis_at), (blocks,), jnp.float32, low / len(cuts), largest / len(cuts))
        return jnp.repeat(jnp.exp(heights), extent[axis_at] // blocks).reshape((-1,) + (1,) * (len(extent) - axis_at - 1))

    loudness = one(*cuts[0])
    for cut in cuts[1:]:
        loudness = loudness * one(*cut)
    return loudness


def split_up(amount, total, most, skew):
    loads = [(1 << 20) // math.isqrt(standing ** skew) + 1 for standing in range(2, amount + 1)]
    spare, counts = total - most - (amount - 1), [1] * (amount - 1)
    while spare > 0:
        movable = [i for i in range(amount - 1) if counts[i] < most]
        whole, remaining = sum([loads[i] for i in movable]), spare
        for i in movable:
            extra = min(most - counts[i], max(1, remaining * loads[i] // whole), spare)
            counts[i] = counts[i] + extra
            spare = spare - extra
    return np.array([most] + counts)


def uneven_parts(own_key, amount, total, most, slope):
    if amount == 2:
        one = jax.random.randint(own_key, (), max(1, total - most), min(most, total - 1) + 1)
        return jnp.stack([one, total - one])
    lengths = jnp.asarray(split_up(amount, total, most, slope), jnp.int32)
    twos = (amount - 1) // 2
    source_of, taker = lengths[1:1 + 2 * twos:2], lengths[2:2 + 2 * twos:2]
    slack = jnp.minimum(source_of - 1, most - taker)
    moved = jax.random.randint(jax.random.fold_in(own_key, 1), (twos,), 0, 1 << 20) % (slack + 1)
    lengths = lengths.at[1:1 + 2 * twos:2].set(source_of - moved).at[2:2 + 2 * twos:2].set(taker + moved)
    return lengths[jax.random.permutation(jax.random.fold_in(own_key, 2), amount)]


def gaussian(key, extent, spread, limit, shards=(), kind=jnp.bfloat16):
    factor_of = levels(key, extent, shards, -0.22, 0.18) if shards else 1.0
    entries = jax.random.normal(key, extent, jnp.float32) * spread * factor_of
    return jnp.minimum(jnp.maximum(entries, -limit), limit).astype(kind)


def gaussian_with(rng, dims, scale, bound, shards, heavy, held_as=jnp.bfloat16):
    drawn = scale * jax.random.normal(rng, dims, jnp.float32)
    if shards:
        drawn = drawn * levels(rng, dims, shards, -0.22, 0.18)
    return jnp.clip(strengthened(drawn, jax.random.fold_in(rng, 3), *heavy), -bound, bound).astype(held_as)


def setup_inputs(seed: int = 0) -> dict:
    seeds = jax.random.split(jax.random.key(seed), 6)
    return {
        "w_cycle": gaussian_with(seeds[0], (IA, KC), (O * V // 8) ** -0.5, 0.109375, ((0, 16), (1, 32)), (1, 0, 32, 2.75)),
        "amplitudes": gaussian(seeds[1], (KO, KO, VCAP, VCAP), 1.0, 6.0, ((0, 32), (2, 16))),
        "occ_count": uneven_parts(seeds[2], IRREPS, O, OCAP, 1).astype(jnp.int32),
        "virt_count": uneven_parts(seeds[3], IRREPS, V, VCAP, 1).astype(jnp.int32),
        "target": jax.random.randint(seeds[4], (1,), 0, IRREPS).astype(jnp.int32),
    }


def pair_valid(occ_count, virt_count, target):
    slot_ids = jnp.arange(IRREPS * OCAP, dtype=jnp.int32)
    irrep_of = slot_ids // OCAP
    labels = jnp.arange(IRREPS, dtype=jnp.int32)
    pick_occ = (irrep_of[:, None] == labels[None, :]).astype(jnp.int32)
    occupied = jnp.sum(pick_occ * occ_count.astype(jnp.int32)[None, :], axis=1)
    partner = jnp.bitwise_xor(irrep_of, target.astype(jnp.int32)[0])
    pick_virt = (partner[:, None] == labels[None, :]).astype(jnp.int32)
    virtual = jnp.sum(pick_virt * virt_count.astype(jnp.int32)[None, :], axis=1)
    column = jnp.arange(VCAP, dtype=jnp.int32)
    valid_pairs = ((slot_ids % OCAP) < occupied)[:, None] & (column[None, :] < virtual[:, None])
    return valid_pairs.astype(jnp.float32)


def reference(w_cycle, amplitudes, occ_count, virt_count, target):
    valid_pairs = pair_valid(occ_count, virt_count, target)
    width_k = KSLICE * VCAP

    def add_block(block_idx, running):
        first_k = (block_idx * KSLICE).astype(jnp.int32)
        amp_rows = lax.dynamic_slice_in_dim(amplitudes, first_k, KSLICE, 0)
        mask_rows = lax.dynamic_slice_in_dim(valid_pairs, first_k, KSLICE, 0)
        masked = amp_rows * mask_rows[:, None, :, None].astype(amp_rows.dtype)
        amp_matrix = jnp.transpose(masked, (0, 2, 1, 3)).reshape(width_k, KC)
        first_col = (block_idx * width_k).astype(jnp.int32)
        w_cols = lax.dynamic_slice_in_dim(w_cycle, first_col, width_k, 1)
        product = jnp.dot(w_cols, amp_matrix, preferred_element_type=jnp.float32)
        rounded = lax.optimization_barrier(product.astype(jnp.bfloat16))
        return running + rounded.astype(jnp.float32)

    summed = lax.fori_loop(0, KO // KSLICE, add_block, jnp.zeros((IA, KC), jnp.float32))
    row_mask = valid_pairs[:IW].reshape(IA)
    col_mask = valid_pairs.reshape(KC)
    return (summed * row_mask[:, None] * col_mask[None, :]).astype(jnp.bfloat16)
```

```python
import jax
import jax.numpy as jnp
from jax import lax
from jax.experimental import pallas as pl
from jax.experimental.pallas import tpu as pltpu
from jax.sharding import Mesh, PartitionSpec as P

IRREPS = 8
OCAP = 24
VCAP = 128
KO = 192
ROWS = 16
TURNS = 8
BLOCK = 48
BF = jnp.bfloat16
F32 = jnp.float32


def scalars():
    return pl.BlockSpec(memory_space=pltpu.SMEM)


def deal_kernel(occ, t_ref, out_ref):
    def put(p, value):
        out_ref[lax.rem(p, ROWS), 0, lax.div(p, ROWS)] = value

    first = jnp.int32(0)
    for h in range(IRREPS):
        def one(s, carry, h=h, first=first):
            slot = h * OCAP + s
            put(first + s, jnp.concatenate([t_ref[0, slot], t_ref[1, slot]], axis=0))
            return carry

        lax.fori_loop(0, occ[h], one, 0)
        first = first + occ[h]

    def rest(p, carry):
        put(p, jnp.zeros((16, VCAP), BF))
        return carry

    lax.fori_loop(first, ROWS * TURNS, rest, 0)


def deal(amplitudes, occ_count):
    return pl.pallas_call(
        deal_kernel,
        grid=(3,),
        in_specs=[scalars(), pl.BlockSpec((2, KO, 8, VCAP), lambda i: (i, 0, 0, 0))],
        out_specs=pl.BlockSpec((ROWS, 1, TURNS, 16, VCAP), lambda i: (0, i, 0, 0, 0)),
        out_shape=jax.ShapeDtypeStruct((ROWS, 3, TURNS, 16, VCAP), BF),
        compiler_params=pltpu.CompilerParams(vmem_limit_bytes=32 << 20),
        name="deal",
    )(occ_count, amplitudes)


def order_kernel(where, occ, virt, target, w_ref, out_ref):
    kc = w_ref.shape[1]
    first_k = where[0] * 6
    irrep = first_k // OCAP
    k_base = first_k - irrep * OCAP
    n_occ = occ[irrep]
    n_virt = virt[jnp.bitwise_xor(irrep, target[0])]
    old = lax.broadcasted_iota(jnp.int32, (kc, kc), 0)
    new = lax.broadcasted_iota(jnp.int32, (kc, kc), 1)
    k, c = old // VCAP, old % VCAP
    goes = (c // 8) * 48 + k * 8 + c % 8
    keep = (goes == new) & (k + k_base < n_occ) & (c < n_virt)
    pick = jnp.where(keep, 1.0, 0.0).astype(BF)
    out_ref[...] = jnp.dot(w_ref[...], pick, preferred_element_type=F32).astype(BF)


def order(w_cycle, col, occ_count, virt_count, target):
    return pl.pallas_call(
        order_kernel,
        in_specs=[scalars()] * 4 + [pl.BlockSpec(memory_space=pltpu.VMEM)],
        out_specs=pl.BlockSpec(memory_space=pltpu.VMEM),
        out_shape=jax.ShapeDtypeStruct(w_cycle.shape, BF),
        compiler_params=pltpu.CompilerParams(vmem_limit_bytes=32 << 20),
        name="order",
    )(col, occ_count, virt_count, target, w_cycle)


def product_kernel(w_ref, t_ref, out_ref):
    depth = w_ref.shape[1]
    right = jnp.concatenate(
        [t_ref[:, 0].reshape(depth, VCAP), t_ref[:, 1].reshape(depth, VCAP)], axis=1
    )
    for x in range(4):
        part = jnp.dot(w_ref[x * 384:(x + 1) * 384, :], right, preferred_element_type=F32)
        for z in range(8):
            at = z * 192 + x * BLOCK
            out_ref[at:at + BLOCK, :] = part[z * BLOCK:(z + 1) * BLOCK].astype(BF)


def product(w_rows, landed):
    rows, depth = w_rows.shape
    width = 2 * VCAP
    return pl.pallas_call(
        product_kernel,
        grid=(TURNS // 2,),
        in_specs=[
            pl.BlockSpec((rows, depth), lambda i: (0, 0)),
            pl.BlockSpec((depth // 16, 2, 16, VCAP), lambda i: (0, i, 0, 0)),
        ],
        out_specs=pl.BlockSpec((rows, width), lambda i: (0, i)),
        out_shape=jax.ShapeDtypeStruct((rows, TURNS * VCAP), BF),
        compiler_params=pltpu.CompilerParams(vmem_limit_bytes=40 << 20),
        name="product",
    )(w_rows, landed)


def first_of(occ, irrep):
    total = jnp.int32(0)
    for h in range(IRREPS):
        total = total + jnp.where(h < irrep, occ[h], 0)
    return total


def send_kernel(where, occ, parts_ref, out_ref):
    mine = where[0]
    first = jnp.int32(0)
    for h in range(IRREPS):
        near = lax.rem(mine - first + 8 * ROWS, ROWS)
        for e in range(2):
            s = near if e == 0 else jnp.where(near < 12, near + ROWS, near)
            turn = jnp.clip((first + s) // ROWS, 0, TURNS - 1)
            at = pl.ds(pl.multiple_of(turn * VCAP, VCAP), VCAP)
            total = parts_ref[0, :, at].astype(F32)
            for x in range(1, 4):
                total = total + parts_ref[x, :, at].astype(F32)
            out_ref[2 * h + e] = total.astype(BF)
        first = first + occ[h]


def send_out(parts, row, occ_count):
    return pl.pallas_call(
        send_kernel,
        in_specs=[scalars()] * 2 + [pl.BlockSpec(memory_space=pltpu.VMEM)],
        out_specs=pl.BlockSpec(memory_space=pltpu.VMEM),
        out_shape=jax.ShapeDtypeStruct((ROWS, BLOCK, VCAP), BF),
        compiler_params=pltpu.CompilerParams(vmem_limit_bytes=32 << 20),
        name="send_out",
    )(row, occ_count, parts)


def place_kernel(where, occ, virt, target, got_ref, out_ref):
    row, col = where[0], where[1]
    irrep, half = row // 2, row % 2
    first = first_of(occ, irrep)
    n_virt = virt[jnp.bitwise_xor(irrep, target[0])]
    line = col * BLOCK + lax.broadcasted_iota(jnp.int32, (BLOCK, VCAP), 0)
    b = lax.broadcasted_iota(jnp.int32, (BLOCK, VCAP), 1)
    inside = (line // VCAP < occ[0]) & (line % VCAP < virt[target[0]]) & (b < n_virt)
    for l in range(12):
        s = half * 12 + l
        block = got_ref[lax.rem(first + s, ROWS)].astype(F32)
        keep = inside & (s < occ[irrep])
        out_ref[:, l * VCAP:(l + 1) * VCAP] = jnp.where(keep, block, 0.0).astype(BF)


def place(got, where, occ_count, virt_count, target):
    return pl.pallas_call(
        place_kernel,
        in_specs=[scalars()] * 4 + [pl.BlockSpec(memory_space=pltpu.VMEM)],
        out_specs=pl.BlockSpec(memory_space=pltpu.VMEM),
        out_shape=jax.ShapeDtypeStruct((BLOCK, 12 * VCAP), BF),
        compiler_params=pltpu.CompilerParams(vmem_limit_bytes=32 << 20),
        name="place",
    )(where, occ_count, virt_count, target, got)


def per_device(w_cycle, amplitudes, occ_count, virt_count, target):
    row = lax.axis_index("y") * 2 + lax.axis_index("core")
    col = lax.axis_index("x") * 8 + lax.axis_index("z")
    row, col = row.astype(jnp.int32), col.astype(jnp.int32)
    line = ("y", "core")
    w_rows = lax.all_gather(
        order(w_cycle, col[None], occ_count, virt_count, target), line, axis=0, tiled=True
    )
    landed = lax.all_to_all(deal(amplitudes, occ_count), line, 0, 0, tiled=True)
    landed = landed.reshape(ROWS * 3, TURNS, 16, VCAP)
    partial = product(w_rows, landed)
    by_z = lax.psum_scatter(partial, "z", scatter_dimension=0, tiled=True)
    by_x = lax.all_to_all(by_z, "x", 0, 0, tiled=True).reshape(4, BLOCK, TURNS * VCAP)
    got = lax.all_to_all(send_out(by_x, row[None], occ_count), line, 0, 0, tiled=True)
    return place(got, jnp.stack([row, col]), occ_count, virt_count, target)


def solution(mesh):
    chips = Mesh(mesh.devices.reshape(8, 2, 4, 8), ("y", "core", "x", "z"))
    row, col = ("y", "core"), ("x", "z")
    placed = (P(row, col), P(col, None, row, None), P(), P(), P())
    return jax.shard_map(
        per_device, mesh=chips, in_specs=placed, out_specs=P(col, row), check_vma=False
    )
```

```python
import functools

import jax
import jax.numpy as jnp
from jax import lax
from jax.experimental import pallas as pl
from jax.experimental.pallas import tpu as pltpu
from jax.sharding import Mesh, PartitionSpec as P

IRREPS = 8
OCAP = 24
VCAP = 128
KO = 192
ROWS = 16
TURNS = 8
EARLY = 6
LATE = TURNS - EARLY
BLOCK = 48
BF = jnp.bfloat16
F32 = jnp.float32


def scalars():
    return pl.BlockSpec(memory_space=pltpu.SMEM)


def slot_table(occ, table):
    first = jnp.int32(0)
    for h in range(IRREPS):
        def one(s, carry, h=h, first=first):
            table[first + s] = h * OCAP + s
            return carry

        lax.fori_loop(0, occ[h], one, 0)
        first = first + occ[h]

    def rest(p, carry):
        table[p] = KO - 1
        return carry

    lax.fori_loop(first, ROWS * TURNS, rest, 0)


def deal_kernel(occ, t_ref, early_ref, late_ref, table):
    @pl.when(pl.program_id(0) == 0)
    def _():
        slot_table(occ, table)

    for turn in range(TURNS):
        for q in range(ROWS):
            slot = table[turn * ROWS + q]
            both = jnp.concatenate([t_ref[0, slot], t_ref[1, slot]], axis=0)
            if turn < EARLY:
                early_ref[q, 0, turn] = both
            else:
                late_ref[q, 0, turn - EARLY] = both


def deal(amplitudes, occ_count):
    def out(turns):
        return pl.BlockSpec((ROWS, 1, turns, 16, VCAP), lambda i: (0, i, 0, 0, 0))

    def shape(turns):
        return jax.ShapeDtypeStruct((ROWS, 3, turns, 16, VCAP), BF)

    return pl.pallas_call(
        deal_kernel,
        grid=(3,),
        in_specs=[scalars(), pl.BlockSpec((2, KO, 8, VCAP), lambda i: (i, 0, 0, 0))],
        out_specs=[out(EARLY), out(LATE)],
        out_shape=[shape(EARLY), shape(LATE)],
        scratch_shapes=[pltpu.SMEM((ROWS * TURNS,), jnp.int32)],
        compiler_params=pltpu.CompilerParams(vmem_limit_bytes=56 << 20),
        name="deal",
    )(occ_count, amplitudes)


def product_kernel(by_reduction, where, occ, virt, target, w_ref, t_ref, out_ref, right):
    depth, width = right.shape

    @pl.when(pl.program_id(0) == 0)
    def _():
        first_k = where[1] * 6
        irrep = first_k // OCAP
        k_base = first_k - irrep * OCAP
        n_occ = occ[irrep]
        n_virt = virt[jnp.bitwise_xor(irrep, target[0])]
        c = lax.broadcasted_iota(jnp.int32, (VCAP, VCAP), 0)
        for turn in range(width // VCAP):
            held = t_ref[:, turn].astype(F32).reshape(ROWS, 3, 2, 8, VCAP)
            for k in range(6):
                limit = jnp.where(k_base + k < n_occ, n_virt, 0)
                value = jnp.where(c < limit, held[:, k // 2, k % 2].reshape(VCAP, VCAP), 0.0)
                right[k * VCAP:(k + 1) * VCAP, turn * VCAP:(turn + 1) * VCAP] = value.astype(BF)

    part = jnp.dot(w_ref[...], right[...], preferred_element_type=F32)
    if by_reduction:
        for z in range(8):
            out_ref[z, 0] = part[z * BLOCK:(z + 1) * BLOCK].astype(BF)
    else:
        out_ref[...] = part.astype(BF)


def product(by_reduction, w_rows, landed, where, occ_count, virt_count, target):
    rows, depth = w_rows.shape
    turns = landed.shape[1]
    width = turns * VCAP
    if by_reduction:
        out_spec = pl.BlockSpec((8, 1, BLOCK, width), lambda i: (0, i, 0, 0))
        out_shape = jax.ShapeDtypeStruct((8, 4, BLOCK, width), BF)
    else:
        out_spec = pl.BlockSpec((rows // 4, width), lambda i: (i, 0))
        out_shape = jax.ShapeDtypeStruct((rows, width), BF)
    out = pl.pallas_call(
        functools.partial(product_kernel, by_reduction),
        grid=(4,),
        in_specs=[scalars()] * 4 + [
            pl.BlockSpec((rows // 4, depth), lambda i: (i, 0)),
            pl.BlockSpec((depth // 16, turns, 16, VCAP), lambda i: (0, 0, 0, 0)),
        ],
        out_specs=out_spec,
        out_shape=out_shape,
        scratch_shapes=[pltpu.VMEM((depth, width), BF)],
        compiler_params=pltpu.CompilerParams(vmem_limit_bytes=56 << 20),
        name="product_early" if by_reduction else "product_late",
    )(where, occ_count, virt_count, target, w_rows, landed)
    return out.reshape(rows, width)


def first_of(occ, irrep):
    total = jnp.int32(0)
    for h in range(IRREPS):
        total = total + jnp.where(h < irrep, occ[h], 0)
    return total


def send_kernel(where, occ, early_ref, late_ref, out_ref, total):
    for turn in range(TURNS):
        parts = early_ref if turn < EARLY else late_ref
        at = (turn if turn < EARLY else turn - EARLY) * VCAP
        added = parts[0, :, at:at + VCAP].astype(F32)
        for x in range(1, parts.shape[0]):
            added = added + parts[x, :, at:at + VCAP].astype(F32)
        total[turn] = added.astype(BF)
    mine = where[0]
    first = jnp.int32(0)
    for h in range(IRREPS):
        near = lax.rem(mine - first + 8 * ROWS, ROWS)
        for e in range(2):
            s = near if e == 0 else jnp.where(near < 12, near + ROWS, near)
            out_ref[2 * h + e] = total[jnp.clip((first + s) // ROWS, 0, TURNS - 1)]
        first = first + occ[h]


def send_out(early, late, where, occ_count):
    return pl.pallas_call(
        send_kernel,
        in_specs=[scalars()] * 2 + [pl.BlockSpec(memory_space=pltpu.VMEM)] * 2,
        out_specs=pl.BlockSpec(memory_space=pltpu.VMEM),
        out_shape=jax.ShapeDtypeStruct((ROWS, BLOCK, VCAP), BF),
        scratch_shapes=[pltpu.VMEM((TURNS, BLOCK, VCAP), BF)],
        compiler_params=pltpu.CompilerParams(vmem_limit_bytes=32 << 20),
        name="send_out",
    )(where, occ_count, early, late)


def place_kernel(where, occ, virt, target, got_ref, out_ref):
    row, col = where[0], where[1]
    irrep, half = row // 2, row % 2
    first = first_of(occ, irrep)
    n_virt = virt[jnp.bitwise_xor(irrep, target[0])]
    line = col * BLOCK + lax.broadcasted_iota(jnp.int32, (BLOCK, VCAP), 0)
    b = lax.broadcasted_iota(jnp.int32, (BLOCK, VCAP), 1)
    inside = (line // VCAP < occ[0]) & (line % VCAP < virt[target[0]]) & (b < n_virt)
    for l in range(12):
        s = half * 12 + l
        block = got_ref[lax.rem(first + s, ROWS)].astype(F32)
        keep = inside & (s < occ[irrep])
        out_ref[:, l * VCAP:(l + 1) * VCAP] = jnp.where(keep, block, 0.0).astype(BF)


def place(got, where, occ_count, virt_count, target):
    return pl.pallas_call(
        place_kernel,
        in_specs=[scalars()] * 4 + [pl.BlockSpec(memory_space=pltpu.VMEM)],
        out_specs=pl.BlockSpec(memory_space=pltpu.VMEM),
        out_shape=jax.ShapeDtypeStruct((BLOCK, 12 * VCAP), BF),
        compiler_params=pltpu.CompilerParams(vmem_limit_bytes=32 << 20),
        name="place",
    )(where, occ_count, virt_count, target, got)


def per_device(w_cycle, amplitudes, occ_count, virt_count, target):
    row = lax.axis_index("y") * 2 + lax.axis_index("core")
    col = lax.axis_index("x") * 8 + lax.axis_index("z")
    where = jnp.stack([row, col]).astype(jnp.int32)
    masks = (where, occ_count, virt_count, target)
    line = ("y", "core")
    w_rows = lax.all_gather(w_cycle, line, axis=0, tiled=True)
    early, late = deal(amplitudes, occ_count)
    early = lax.all_to_all(early, line, 0, 0, tiled=True).reshape(ROWS * 3, EARLY, 16, VCAP)
    early = product(True, w_rows, early, *masks)
    early, late = lax.optimization_barrier((early, late))
    early = lax.psum_scatter(early, "z", scatter_dimension=0, tiled=True)
    late = lax.all_to_all(late, line, 0, 0, tiled=True).reshape(ROWS * 3, LATE, 16, VCAP)
    late = product(False, w_rows, late, *masks)
    late = lax.all_to_all(late, ("x", "z"), 0, 0, tiled=True).reshape(32, BLOCK, LATE * VCAP)
    early = lax.all_to_all(early, "x", 0, 0, tiled=True).reshape(4, BLOCK, EARLY * VCAP)
    got = lax.all_to_all(send_out(early, late, where, occ_count), line, 0, 0, tiled=True)
    return place(got, *masks)


def solution(mesh):
    chips = Mesh(mesh.devices.reshape(8, 2, 4, 8), ("y", "core", "x", "z"))
    row, col = ("y", "core"), ("x", "z")
    placed = (P(row, col), P(col, None, row, None), P(), P(), P())
    return jax.shard_map(
        per_device, mesh=chips, in_specs=placed, out_specs=P(col, row), check_vma=False
    )
```

```python
import jax
import jax.numpy as jnp
from jax import lax
from jax.experimental import pallas as pl
from jax.experimental.pallas import tpu as pltpu
from jax.sharding import Mesh, PartitionSpec as P

IRREPS = 8
OCAP = 24
VCAP = 128
KO = 192
ROWS = 16
TURNS = 8
BLOCK = 48
BF = jnp.bfloat16
F32 = jnp.float32


def scalars():
    return pl.BlockSpec(memory_space=pltpu.SMEM)


def slot_table(occ, table):
    first = jnp.int32(0)
    for h in range(IRREPS):
        def one(s, carry, h=h, first=first):
            table[first + s] = h * OCAP + s
            return carry

        lax.fori_loop(0, occ[h], one, 0)
        first = first + occ[h]

    def rest(p, carry):
        table[p] = KO - 1
        return carry

    lax.fori_loop(first, ROWS * TURNS, rest, 0)


def deal_kernel(occ, t_ref, out_ref, table):
    @pl.when(pl.program_id(0) == 0)
    def _():
        slot_table(occ, table)

    for turn in range(TURNS):
        for q in range(ROWS):
            slot = table[turn * ROWS + q]
            out_ref[q, 0, turn] = t_ref[0, slot]
            out_ref[q, 1, turn] = t_ref[1, slot]


def deal(amplitudes, occ_count):
    return pl.pallas_call(
        deal_kernel,
        grid=(3,),
        in_specs=[scalars(), pl.BlockSpec((2, KO, 8, VCAP), lambda i: (i, 0, 0, 0))],
        out_specs=pl.BlockSpec((ROWS, 2, TURNS, 8, VCAP), lambda i: (0, i, 0, 0, 0)),
        out_shape=jax.ShapeDtypeStruct((ROWS, 6, TURNS, 8, VCAP), BF),
        scratch_shapes=[pltpu.SMEM((ROWS * TURNS,), jnp.int32)],
        compiler_params=pltpu.CompilerParams(vmem_limit_bytes=56 << 20),
        name="deal",
    )(occ_count, amplitudes)


def repack_kernel(where, occ, virt, target, t_ref, out_ref):
    first_k = where[1] * 6
    irrep = first_k // OCAP
    k_base = first_k - irrep * OCAP
    n_occ = occ[irrep]
    n_virt = virt[jnp.bitwise_xor(irrep, target[0])]
    c = lax.broadcasted_iota(jnp.int32, (VCAP, VCAP), 0)
    for turn in range(t_ref.shape[1]):
        held = t_ref[:, turn].astype(F32).reshape(ROWS, 6, 8, VCAP)
        for k in range(6):
            limit = jnp.where(k_base + k < n_occ, n_virt, 0)
            value = jnp.where(c < limit, held[:, k].reshape(VCAP, VCAP), 0.0)
            out_ref[k * VCAP:(k + 1) * VCAP, turn * VCAP:(turn + 1) * VCAP] = value.astype(BF)


def repack(landed, where, occ_count, virt_count, target):
    return pl.pallas_call(
        repack_kernel,
        grid=(TURNS // 2,),
        in_specs=[scalars()] * 4 + [pl.BlockSpec((ROWS * 6, 2, 8, VCAP), lambda i: (0, i, 0, 0))],
        out_specs=pl.BlockSpec((6 * VCAP, 2 * VCAP), lambda i: (0, i)),
        out_shape=jax.ShapeDtypeStruct((6 * VCAP, TURNS * VCAP), BF),
        compiler_params=pltpu.CompilerParams(vmem_limit_bytes=56 << 20),
        name="repack",
    )(where, occ_count, virt_count, target, landed)


def product_kernel(w_ref, t_ref, out_ref):
    part = jnp.dot(w_ref[...], t_ref[...], preferred_element_type=F32)
    for z in range(8):
        out_ref[z, 0] = part[z * BLOCK:(z + 1) * BLOCK].astype(BF)


def product(w_rows, t_rows):
    rows, depth = w_rows.shape
    width = t_rows.shape[1]
    out = pl.pallas_call(
        product_kernel,
        grid=(4,),
        in_specs=[
            pl.BlockSpec((rows // 4, depth), lambda i: (i, 0)),
            pl.BlockSpec((depth, width), lambda i: (0, 0)),
        ],
        out_specs=pl.BlockSpec((8, 1, BLOCK, width), lambda i: (0, i, 0, 0)),
        out_shape=jax.ShapeDtypeStruct((8, 4, BLOCK, width), BF),
        compiler_params=pltpu.CompilerParams(vmem_limit_bytes=56 << 20),
        name="product",
    )(w_rows, t_rows)
    return out.reshape(rows, width)


def first_of(occ, irrep):
    total = jnp.int32(0)
    for h in range(IRREPS):
        total = total + jnp.where(h < irrep, occ[h], 0)
    return total


def send_kernel(where, occ, parts_ref, out_ref, total):
    for turn in range(TURNS):
        at = turn * VCAP
        added = parts_ref[0, :, at:at + VCAP].astype(F32)
        for x in range(1, 4):
            added = added + parts_ref[x, :, at:at + VCAP].astype(F32)
        total[turn] = added.astype(BF)
    mine = where[0]
    first = jnp.int32(0)
    for h in range(IRREPS):
        near = lax.rem(mine - first + 8 * ROWS, ROWS)
        for e in range(2):
            s = near if e == 0 else jnp.where(near < 12, near + ROWS, near)
            out_ref[2 * h + e] = total[jnp.clip((first + s) // ROWS, 0, TURNS - 1)]
        first = first + occ[h]


def send_out(parts, where, occ_count):
    return pl.pallas_call(
        send_kernel,
        in_specs=[scalars()] * 2 + [pl.BlockSpec(memory_space=pltpu.VMEM)],
        out_specs=pl.BlockSpec(memory_space=pltpu.VMEM),
        out_shape=jax.ShapeDtypeStruct((ROWS, BLOCK, VCAP), BF),
        scratch_shapes=[pltpu.VMEM((TURNS, BLOCK, VCAP), BF)],
        compiler_params=pltpu.CompilerParams(vmem_limit_bytes=32 << 20),
        name="send_out",
    )(where, occ_count, parts)


def place_kernel(where, occ, virt, target, got_ref, out_ref):
    row, col = where[0], where[1]
    irrep, half = row // 2, row % 2
    first = first_of(occ, irrep)
    n_virt = virt[jnp.bitwise_xor(irrep, target[0])]
    line = col * BLOCK + lax.broadcasted_iota(jnp.int32, (BLOCK, VCAP), 0)
    b = lax.broadcasted_iota(jnp.int32, (BLOCK, VCAP), 1)
    inside = (line // VCAP < occ[0]) & (line % VCAP < virt[target[0]]) & (b < n_virt)
    for l in range(12):
        s = half * 12 + l
        block = got_ref[lax.rem(first + s, ROWS)].astype(F32)
        keep = inside & (s < occ[irrep])
        out_ref[:, l * VCAP:(l + 1) * VCAP] = jnp.where(keep, block, 0.0).astype(BF)


def place(got, where, occ_count, virt_count, target):
    return pl.pallas_call(
        place_kernel,
        in_specs=[scalars()] * 4 + [pl.BlockSpec(memory_space=pltpu.VMEM)],
        out_specs=pl.BlockSpec(memory_space=pltpu.VMEM),
        out_shape=jax.ShapeDtypeStruct((BLOCK, 12 * VCAP), BF),
        compiler_params=pltpu.CompilerParams(vmem_limit_bytes=32 << 20),
        name="place",
    )(where, occ_count, virt_count, target, got)


def per_device(w_cycle, amplitudes, occ_count, virt_count, target):
    row = lax.axis_index("y") * 2 + lax.axis_index("core")
    col = lax.axis_index("x") * 8 + lax.axis_index("z")
    where = jnp.stack([row, col]).astype(jnp.int32)
    masks = (where, occ_count, virt_count, target)
    line = ("y", "core")
    w_rows = lax.all_gather(w_cycle, line, axis=0, tiled=True)
    landed = lax.all_to_all(deal(amplitudes, occ_count), line, 0, 0, tiled=True)
    t_rows = repack(landed.reshape(ROWS * 6, TURNS, 8, VCAP), *masks)
    partial = product(w_rows, t_rows)
    by_z = lax.psum_scatter(partial, "z", scatter_dimension=0, tiled=True)
    by_x = lax.all_to_all(by_z, "x", 0, 0, tiled=True).reshape(4, BLOCK, TURNS * VCAP)
    got = lax.all_to_all(send_out(by_x, where, occ_count), line, 0, 0, tiled=True)
    return place(got, *masks)


def solution(mesh):
    chips = Mesh(mesh.devices.reshape(8, 2, 4, 8), ("y", "core", "x", "z"))
    row, col = ("y", "core"), ("x", "z")
    placed = (P(row, col), P(col, None, row, None), P(), P(), P())
    return jax.shard_map(
        per_device, mesh=chips, in_specs=placed, out_specs=P(col, row), check_vma=False
    )
```

```python
import functools

import jax
import jax.numpy as jnp
from jax import lax
from jax.experimental import pallas as pl
from jax.experimental.pallas import tpu as pltpu
from jax.sharding import Mesh, PartitionSpec as P

IRREPS = 8
OCAP = 24
VCAP = 128
KO = 192
ROWS = 16
SIZES = (5, 6, 8)
STEP = 6
BLOCK = 48
BF = jnp.bfloat16
F32 = jnp.float32


def scalars():
    return pl.BlockSpec(memory_space=pltpu.SMEM)


def columns_of(occ, virt, target, irrep):
    return virt[jnp.bitwise_xor(irrep, target[0])]


def first_column(occ, virt, target, irrep):
    total = jnp.int32(0)
    for h in range(IRREPS):
        total = total + jnp.where(h < irrep, occ[h] * columns_of(occ, virt, target, h), 0)
    return total


def deal_kernel(occ, virt, target, t_ref, out_ref, held, sem):
    copies = [
        pltpu.make_async_copy(
            t_ref.at[:, h * OCAP:(h + 1) * OCAP], held.at[:, h * OCAP:(h + 1) * OCAP], sem.at[h]
        )
        for h in range(IRREPS)
    ]
    for copy in copies:
        copy.start()
    lane = lax.broadcasted_iota(jnp.int32, (48, VCAP), 1)

    def put(p, value):
        out_ref[jnp.bitwise_and(p, 15), :, lax.shift_right_logical(p, 4)] = (
            value.astype(BF).reshape(6, 8, VCAP)
        )

    current = jnp.zeros((48, VCAP), F32)
    first = jnp.int32(0)
    for h in range(IRREPS):
        copies[h].wait()
        many = occ[h]
        wide = columns_of(occ, virt, target, h)

        def some(g, current, h=h, first=first, many=many, wide=wide):
            for u in range(STEP):
                s = g * STEP + u
                at = first + jnp.minimum(s, many) * wide
                shift = jnp.bitwise_and(at, 127)
                value = held[:, h * OCAP + s].astype(F32).reshape(48, VCAP)
                value = pltpu.roll(value, shift, 1)
                current = jnp.where(lane >= shift, value, current)
                put(lax.shift_right_logical(at, 7), current)
                current = jnp.where((s < many) & (shift + wide >= VCAP), value, current)
            return current

        current = lax.fori_loop(0, (many + STEP - 1) // STEP, some, current)
        first = first + many * wide
    put(lax.shift_right_logical(first, 7), current)


def deal(turns, amplitudes, occ_count, virt_count, target):
    return pl.pallas_call(
        deal_kernel,
        in_specs=[scalars()] * 3 + [pl.BlockSpec(memory_space=pl.ANY)],
        out_specs=pl.BlockSpec(memory_space=pltpu.VMEM),
        out_shape=jax.ShapeDtypeStruct((ROWS, 6, turns, 8, VCAP), BF),
        scratch_shapes=[pltpu.VMEM((6, KO, 8, VCAP), BF), pltpu.SemaphoreType.DMA((IRREPS,))],
        compiler_params=pltpu.CompilerParams(vmem_limit_bytes=56 << 20),
        name="deal",
    )(occ_count, virt_count, target, amplitudes)


def repack_kernel(where, occ, virt, target, t_ref, out_ref):
    first_k = where[1] * 6
    irrep = first_k // OCAP
    k_base = first_k - irrep * OCAP
    n_occ = occ[irrep]
    n_virt = columns_of(occ, virt, target, irrep)
    c = lax.broadcasted_iota(jnp.int32, (VCAP, VCAP), 0)
    for turn in range(t_ref.shape[1]):
        held = t_ref[:, turn].astype(F32).reshape(ROWS, 6, 8, VCAP)
        for k in range(6):
            limit = jnp.where(k_base + k < n_occ, n_virt, 0)
            value = jnp.where(c < limit, held[:, k].reshape(VCAP, VCAP), 0.0)
            out_ref[k * VCAP:(k + 1) * VCAP, turn * VCAP:(turn + 1) * VCAP] = value.astype(BF)


def repack(landed, where, occ_count, virt_count, target):
    turns = landed.shape[1]
    return pl.pallas_call(
        repack_kernel,
        in_specs=[scalars()] * 4 + [pl.BlockSpec(memory_space=pltpu.VMEM)],
        out_specs=pl.BlockSpec(memory_space=pltpu.VMEM),
        out_shape=jax.ShapeDtypeStruct((6 * VCAP, turns * VCAP), BF),
        compiler_params=pltpu.CompilerParams(vmem_limit_bytes=24 << 20),
        name="repack",
    )(where, occ_count, virt_count, target, landed)


def product_kernel(w_ref, t_ref, out_ref, w_held, t_held, out_held, w_sem, t_sem, out_sem):
    tall = w_ref.shape[0] // 4
    t_copy = pltpu.make_async_copy(t_ref, t_held, t_sem)
    t_copy.start()
    w_copies = [
        pltpu.make_async_copy(
            w_ref.at[x * tall:(x + 1) * tall], w_held.at[x * tall:(x + 1) * tall], w_sem.at[x]
        )
        for x in range(4)
    ]
    for copy in w_copies:
        copy.start()
    t_copy.wait()
    out_copies = []
    for x in range(4):
        w_copies[x].wait()
        part = jnp.dot(
            w_held[x * tall:(x + 1) * tall, :], t_held[...], preferred_element_type=F32
        )
        for z in range(8):
            out_held[x, z] = part[z * BLOCK:(z + 1) * BLOCK].astype(BF)
        copy = pltpu.make_async_copy(out_held.at[x], out_ref.at[:, x], out_sem.at[x])
        copy.start()
        out_copies.append(copy)
    for copy in out_copies:
        copy.wait()


def product(w_rows, t_rows):
    rows, depth = w_rows.shape
    width = t_rows.shape[1]
    out = pl.pallas_call(
        product_kernel,
        in_specs=[pl.BlockSpec(memory_space=pl.ANY)] * 2,
        out_specs=pl.BlockSpec(memory_space=pl.ANY),
        out_shape=jax.ShapeDtypeStruct((8, 4, BLOCK, width), BF),
        scratch_shapes=[
            pltpu.VMEM((rows, depth), BF),
            pltpu.VMEM((depth, width), BF),
            pltpu.VMEM((4, 8, BLOCK, width), BF),
            pltpu.SemaphoreType.DMA((4,)),
            pltpu.SemaphoreType.DMA,
            pltpu.SemaphoreType.DMA((4,)),
        ],
        compiler_params=pltpu.CompilerParams(vmem_limit_bytes=56 << 20),
        name="product",
    )(w_rows, t_rows)
    return out.reshape(rows, width)


def send_kernel(where, occ, virt, target, parts_ref, out_ref, total):
    turns = total.shape[0]
    for turn in range(turns):
        at = turn * VCAP
        added = parts_ref[0, :, at:at + VCAP].astype(F32)
        for x in range(1, 4):
            added = added + parts_ref[x, :, at:at + VCAP].astype(F32)
        total[turn] = added.astype(BF)
    mine = where[0]
    first = jnp.int32(0)
    for h in range(IRREPS):
        wide = columns_of(occ, virt, target, h)
        for e in range(2):
            begin = lax.shift_right_logical(first + 12 * e * wide, 7)
            p = begin + jnp.bitwise_and(mine - begin + 16 * ROWS, 15)
            out_ref[2 * h + e] = total[jnp.minimum(lax.shift_right_logical(p, 4), turns - 1)]
        first = first + occ[h] * wide


def send_out(parts, where, occ_count, virt_count, target):
    return pl.pallas_call(
        send_kernel,
        in_specs=[scalars()] * 4 + [pl.BlockSpec(memory_space=pltpu.VMEM)],
        out_specs=pl.BlockSpec(memory_space=pltpu.VMEM),
        out_shape=jax.ShapeDtypeStruct((ROWS, BLOCK, VCAP), BF),
        scratch_shapes=[pltpu.VMEM((parts.shape[2] // VCAP, BLOCK, VCAP), BF)],
        compiler_params=pltpu.CompilerParams(vmem_limit_bytes=24 << 20),
        name="send_out",
    )(where, occ_count, virt_count, target, parts)


def place_kernel(where, occ, virt, target, got_ref, out_ref):
    row, col = where[0], where[1]
    irrep, half = row // 2, row % 2
    first = first_column(occ, virt, target, irrep)
    wide = columns_of(occ, virt, target, irrep)
    line = col * BLOCK + lax.broadcasted_iota(jnp.int32, (BLOCK, VCAP), 0)
    b = lax.broadcasted_iota(jnp.int32, (BLOCK, VCAP), 1)
    inside = (line // VCAP < occ[0]) & (line % VCAP < virt[target[0]]) & (b < wide)
    for l in range(12):
        s = half * 12 + l
        at = first + s * wide
        p = lax.shift_right_logical(at, 7)
        shift = jnp.bitwise_and(at, 127)
        here = got_ref[jnp.bitwise_and(p, 15)].astype(F32)
        after = got_ref[jnp.bitwise_and(p + 1, 15)].astype(F32)
        block = jnp.where(b >= shift, here, after)
        block = pltpu.roll(block, jnp.bitwise_and(VCAP - shift, 127), 1)
        keep = inside & (s < occ[irrep])
        out_ref[:, l * VCAP:(l + 1) * VCAP] = jnp.where(keep, block, 0.0).astype(BF)


def place(got, where, occ_count, virt_count, target):
    return pl.pallas_call(
        place_kernel,
        in_specs=[scalars()] * 4 + [pl.BlockSpec(memory_space=pltpu.VMEM)],
        out_specs=pl.BlockSpec(memory_space=pltpu.VMEM),
        out_shape=jax.ShapeDtypeStruct((BLOCK, 12 * VCAP), BF),
        compiler_params=pltpu.CompilerParams(vmem_limit_bytes=32 << 20),
        name="place",
    )(where, occ_count, virt_count, target, got)


def contract(turns, where, w_cycle, amplitudes, occ_count, virt_count, target):
    masks = (where, occ_count, virt_count, target)
    line = ("y", "core")
    w_rows = lax.all_gather(w_cycle, line, axis=0, tiled=True)
    dealt = deal(turns, amplitudes, occ_count, virt_count, target)
    landed = lax.all_to_all(dealt, line, 0, 0, tiled=True)
    t_rows = repack(landed.reshape(ROWS * 6, turns, 8, VCAP), *masks)
    partial = product(w_rows, t_rows)
    by_z = lax.psum_scatter(partial, "z", scatter_dimension=0, tiled=True)
    by_x = lax.all_to_all(by_z, "x", 0, 0, tiled=True).reshape(4, BLOCK, turns * VCAP)
    got = lax.all_to_all(send_out(by_x, *masks), line, 0, 0, tiled=True)
    return place(got, *masks)


def per_device(w_cycle, amplitudes, occ_count, virt_count, target):
    row = lax.axis_index("y") * 2 + lax.axis_index("core")
    col = lax.axis_index("x") * 8 + lax.axis_index("z")
    where = jnp.stack([row, col]).astype(jnp.int32)
    irreps = jnp.arange(IRREPS, dtype=jnp.int32)
    meets = jnp.bitwise_xor(irreps, target)[:, None] == irreps[None, :]
    pairs = jnp.sum(jnp.where(meets, occ_count[:, None] * virt_count[None, :], 0))
    case = sum((pairs > (ROWS * turns - 1) * VCAP).astype(jnp.int32) for turns in SIZES[:-1])
    return lax.switch(
        case,
        [functools.partial(contract, turns) for turns in SIZES],
        where, w_cycle, amplitudes, occ_count, virt_count, target,
    )


def solution(mesh):
    chips = Mesh(mesh.devices.reshape(8, 2, 4, 8), ("y", "core", "x", "z"))
    row, col = ("y", "core"), ("x", "z")
    placed = (P(row, col), P(col, None, row, None), P(), P(), P())
    return jax.shard_map(
        per_device, mesh=chips, in_specs=placed, out_specs=P(col, row), check_vma=False
    )
```

```python
import functools

import jax
import jax.numpy as jnp
from jax import lax
from jax.experimental import pallas as pl
from jax.experimental.pallas import tpu as pltpu
from jax.sharding import Mesh, PartitionSpec as P

IRREPS = 8
OCAP = 24
VCAP = 128
KO = 192
ROWS = 16
SIZES = (5, 6, 8)
STEP = 12
BLOCK = 48
BF = jnp.bfloat16
F32 = jnp.float32


def scalars():
    return pl.BlockSpec(memory_space=pltpu.SMEM)


def columns_of(occ, virt, target, irrep):
    return virt[jnp.bitwise_xor(irrep, target[0])]


def first_column(occ, virt, target, irrep):
    total = jnp.int32(0)
    for h in range(IRREPS):
        total = total + jnp.where(h < irrep, occ[h] * columns_of(occ, virt, target, h), 0)
    return total


def deal_kernel(occ, virt, target, t_ref, out_ref, held, sem):
    copies = [
        pltpu.make_async_copy(
            t_ref.at[:, h * OCAP:(h + 1) * OCAP], held.at[:, h * OCAP:(h + 1) * OCAP], sem.at[h]
        )
        for h in range(IRREPS)
    ]
    for copy in copies:
        copy.start()
    lane = lax.broadcasted_iota(jnp.int32, (48, VCAP), 1)

    def put(p, value):
        out_ref[jnp.bitwise_and(p, 15), :, lax.shift_right_logical(p, 4)] = (
            value.astype(BF).reshape(6, 8, VCAP)
        )

    current = jnp.zeros((48, VCAP), F32)
    first = jnp.int32(0)
    for h in range(IRREPS):
        copies[h].wait()
        many = occ[h]
        wide = columns_of(occ, virt, target, h)

        def some(g, current, h=h, first=first, many=many, wide=wide):
            for u in range(STEP):
                s = g * STEP + u
                at = first + jnp.minimum(s, many) * wide
                shift = jnp.bitwise_and(at, 127)
                value = held[:, h * OCAP + s].astype(F32).reshape(48, VCAP)
                value = pltpu.roll(value, shift, 1)
                current = jnp.where(lane >= shift, value, current)
                put(lax.shift_right_logical(at, 7), current)
                current = jnp.where((s < many) & (shift + wide >= VCAP), value, current)
            return current

        current = lax.fori_loop(0, (many + STEP - 1) // STEP, some, current)
        first = first + many * wide
    put(lax.shift_right_logical(first, 7), current)


def deal(turns, amplitudes, occ_count, virt_count, target):
    return pl.pallas_call(
        deal_kernel,
        in_specs=[scalars()] * 3 + [pl.BlockSpec(memory_space=pltpu.HBM)],
        out_specs=pl.BlockSpec(memory_space=pltpu.VMEM),
        out_shape=jax.ShapeDtypeStruct((ROWS, 6, turns, 8, VCAP), BF),
        scratch_shapes=[pltpu.VMEM((6, KO, 8, VCAP), BF), pltpu.SemaphoreType.DMA((IRREPS,))],
        compiler_params=pltpu.CompilerParams(vmem_limit_bytes=24 << 20),
        name="deal",
    )(occ_count, virt_count, target, amplitudes)


def repack_kernel(where, occ, virt, target, t_ref, out_ref):
    first_k = where[1] * 6
    irrep = first_k // OCAP
    k_base = first_k - irrep * OCAP
    n_occ = occ[irrep]
    n_virt = columns_of(occ, virt, target, irrep)
    c = lax.broadcasted_iota(jnp.int32, (VCAP, VCAP), 0)
    for turn in range(t_ref.shape[1]):
        held = t_ref[:, turn].astype(F32).reshape(ROWS, 6, 8, VCAP)
        for k in range(6):
            limit = jnp.where(k_base + k < n_occ, n_virt, 0)
            value = jnp.where(c < limit, held[:, k].reshape(VCAP, VCAP), 0.0)
            out_ref[k * VCAP:(k + 1) * VCAP, turn * VCAP:(turn + 1) * VCAP] = value.astype(BF)


def repack(landed, where, occ_count, virt_count, target):
    turns = landed.shape[1]
    return pl.pallas_call(
        repack_kernel,
        in_specs=[scalars()] * 4 + [pl.BlockSpec(memory_space=pltpu.VMEM)],
        out_specs=pl.BlockSpec(memory_space=pltpu.VMEM),
        out_shape=jax.ShapeDtypeStruct((6 * VCAP, turns * VCAP), BF),
        compiler_params=pltpu.CompilerParams(vmem_limit_bytes=24 << 20),
        name="repack",
    )(where, occ_count, virt_count, target, landed)


def product_kernel(where, own_ref, other_ref, t_ref, out_ref, held, sem):
    core = lax.rem(where[0], 2)
    tall = 8 * BLOCK
    copies = []
    for part, (ref, of_core) in enumerate(((own_ref, core), (other_ref, 1 - core))):
        for pair in range(2):
            value = jnp.dot(
                ref[pair * tall:(pair + 1) * tall, :], t_ref[...], preferred_element_type=F32
            )
            for n in range(4):
                at = 4 * (2 * part + pair) + n
                y = 4 * pair + n
                for i in range(2):
                    begin = (2 * n + i) * BLOCK
                    held[at, i] = value[begin:begin + BLOCK].astype(BF)
                copy = pltpu.make_async_copy(
                    held.at[at], out_ref.at[pl.ds(4 * (y % 2) + 2 * of_core, 2), y // 2], sem.at[at]
                )
                copy.start()
                copies.append(copy)
    for copy in copies:
        copy.wait()


def product(own, other, t_rows, where):
    rows, depth = own.shape
    width = t_rows.shape[1]
    out = pl.pallas_call(
        product_kernel,
        in_specs=[scalars()] + [pl.BlockSpec(memory_space=pltpu.VMEM)] * 3,
        out_specs=pl.BlockSpec(memory_space=pltpu.HBM),
        out_shape=jax.ShapeDtypeStruct((8, 4, BLOCK, width), BF),
        scratch_shapes=[pltpu.VMEM((16, 2, BLOCK, width), BF), pltpu.SemaphoreType.DMA((16,))],
        compiler_params=pltpu.CompilerParams(vmem_limit_bytes=24 << 20),
        name="product",
    )(where, own, other, t_rows)
    return out.reshape(2 * rows, width)


def send_kernel(where, occ, virt, target, parts_ref, out_ref, total):
    turns = total.shape[0]
    for turn in range(turns):
        at = turn * VCAP
        added = parts_ref[0, :, at:at + VCAP].astype(F32)
        for x in range(1, 4):
            added = added + parts_ref[x, :, at:at + VCAP].astype(F32)
        total[turn] = added.astype(BF)
    mine = where[0]
    first = jnp.int32(0)
    for h in range(IRREPS):
        wide = columns_of(occ, virt, target, h)
        for e in range(2):
            begin = lax.shift_right_logical(first + 12 * e * wide, 7)
            p = begin + jnp.bitwise_and(mine - begin + 16 * ROWS, 15)
            out_ref[2 * h + e] = total[jnp.minimum(lax.shift_right_logical(p, 4), turns - 1)]
        first = first + occ[h] * wide


def send_out(parts, where, occ_count, virt_count, target):
    return pl.pallas_call(
        send_kernel,
        in_specs=[scalars()] * 4 + [pl.BlockSpec(memory_space=pltpu.VMEM)],
        out_specs=pl.BlockSpec(memory_space=pltpu.VMEM),
        out_shape=jax.ShapeDtypeStruct((ROWS, BLOCK, VCAP), BF),
        scratch_shapes=[pltpu.VMEM((parts.shape[2] // VCAP, BLOCK, VCAP), BF)],
        compiler_params=pltpu.CompilerParams(vmem_limit_bytes=24 << 20),
        name="send_out",
    )(where, occ_count, virt_count, target, parts)


def place_kernel(where, occ, virt, target, got_ref, out_ref):
    row, col = where[0], where[1]
    irrep, half = row // 2, row % 2
    first = first_column(occ, virt, target, irrep)
    wide = columns_of(occ, virt, target, irrep)
    line = col * BLOCK + lax.broadcasted_iota(jnp.int32, (BLOCK, VCAP), 0)
    b = lax.broadcasted_iota(jnp.int32, (BLOCK, VCAP), 1)
    inside = (line // VCAP < occ[0]) & (line % VCAP < virt[target[0]]) & (b < wide)
    for l in range(12):
        s = half * 12 + l
        at = first + s * wide
        p = lax.shift_right_logical(at, 7)
        shift = jnp.bitwise_and(at, 127)
        here = got_ref[jnp.bitwise_and(p, 15)].astype(F32)
        after = got_ref[jnp.bitwise_and(p + 1, 15)].astype(F32)
        block = jnp.where(b >= shift, here, after)
        block = pltpu.roll(block, jnp.bitwise_and(VCAP - shift, 127), 1)
        keep = inside & (s < occ[irrep])
        out_ref[:, l * VCAP:(l + 1) * VCAP] = jnp.where(keep, block, 0.0).astype(BF)


def place(got, where, occ_count, virt_count, target):
    return pl.pallas_call(
        place_kernel,
        in_specs=[scalars()] * 4 + [pl.BlockSpec(memory_space=pltpu.VMEM)],
        out_specs=pl.BlockSpec(memory_space=pltpu.VMEM),
        out_shape=jax.ShapeDtypeStruct((BLOCK, 12 * VCAP), BF),
        compiler_params=pltpu.CompilerParams(vmem_limit_bytes=24 << 20),
        name="place",
    )(where, occ_count, virt_count, target, got)


def contract(turns, where, w_cycle, amplitudes, occ_count, virt_count, target):
    masks = (where, occ_count, virt_count, target)
    line = ("y", "core")
    own = lax.all_gather(w_cycle, "y", axis=0, tiled=True)
    dealt = deal(turns, amplitudes, occ_count, virt_count, target)
    landed = lax.all_to_all(dealt, line, 0, 0, tiled=True)
    own, landed = lax.optimization_barrier((own, landed))
    other = lax.ppermute(own, "core", [(0, 1), (1, 0)])
    t_rows = repack(landed.reshape(ROWS * 6, turns, 8, VCAP), *masks)
    partial = product(own, other, t_rows, where)
    by_z = lax.psum_scatter(partial, "z", scatter_dimension=0, tiled=True)
    by_x = lax.all_to_all(by_z, "x", 0, 0, tiled=True).reshape(4, BLOCK, turns * VCAP)
    return lax.all_to_all(send_out(by_x, *masks), line, 0, 0, tiled=True)


def per_device(w_cycle, amplitudes, occ_count, virt_count, target):
    row = lax.axis_index("y") * 2 + lax.axis_index("core")
    col = lax.axis_index("x") * 8 + lax.axis_index("z")
    where = jnp.stack([row, col]).astype(jnp.int32)
    irreps = jnp.arange(IRREPS, dtype=jnp.int32)
    meets = jnp.bitwise_xor(irreps, target)[:, None] == irreps[None, :]
    pairs = jnp.sum(jnp.where(meets, occ_count[:, None] * virt_count[None, :], 0))
    case = sum((pairs > (ROWS * turns - 1) * VCAP).astype(jnp.int32) for turns in SIZES[:-1])
    got = lax.switch(
        case,
        [functools.partial(contract, turns) for turns in SIZES],
        where, w_cycle, amplitudes, occ_count, virt_count, target,
    )
    return place(got, where, occ_count, virt_count, target)


def solution(mesh):
    chips = Mesh(mesh.devices.reshape(8, 2, 4, 8), ("y", "core", "x", "z"))
    row, col = ("y", "core"), ("x", "z")
    placed = (P(row, col), P(col, None, row, None), P(), P(), P())
    return jax.shard_map(
        per_device, mesh=chips, in_specs=placed, out_specs=P(col, row), check_vma=False
    )
```

```python
import functools

import jax
import jax.numpy as jnp
from jax import lax
from jax.experimental import pallas as pl
from jax.experimental.pallas import tpu as pltpu
from jax.sharding import Mesh, PartitionSpec as P

IRREPS = 8
OCAP = 24
VCAP = 128
KO = 192
ROWS = 16
SIZES = (5, 6, 8)
STEP = 12
BLOCK = 48
BF = jnp.bfloat16
F32 = jnp.float32


def scalars():
    return pl.BlockSpec(memory_space=pltpu.SMEM)


def columns_of(occ, virt, target, irrep):
    return virt[jnp.bitwise_xor(irrep, target[0])]


def first_column(occ, virt, target, irrep):
    total = jnp.int32(0)
    for h in range(IRREPS):
        total = total + jnp.where(h < irrep, occ[h] * columns_of(occ, virt, target, h), 0)
    return total


def deal_kernel(occ, virt, target, t_ref, out_ref, held, sem):
    copies = [
        pltpu.make_async_copy(
            t_ref.at[:, h * OCAP:(h + 1) * OCAP], held.at[:, h * OCAP:(h + 1) * OCAP], sem.at[h]
        )
        for h in range(IRREPS)
    ]
    for copy in copies:
        copy.start()
    lane = lax.broadcasted_iota(jnp.int32, (48, VCAP), 1)

    def put(p, value):
        out_ref[jnp.bitwise_and(p, 15), :, lax.shift_right_logical(p, 4)] = (
            value.astype(BF).reshape(6, 8, VCAP)
        )

    current = jnp.zeros((48, VCAP), F32)
    first = jnp.int32(0)
    for h in range(IRREPS):
        copies[h].wait()
        many = occ[h]
        wide = columns_of(occ, virt, target, h)

        def some(g, current, h=h, first=first, many=many, wide=wide):
            for u in range(STEP):
                s = g * STEP + u
                at = first + jnp.minimum(s, many) * wide
                shift = jnp.bitwise_and(at, 127)
                value = held[:, h * OCAP + s].astype(F32).reshape(48, VCAP)
                value = pltpu.roll(value, shift, 1)
                current = jnp.where(lane >= shift, value, current)
                put(lax.shift_right_logical(at, 7), current)
                current = jnp.where((s < many) & (shift + wide >= VCAP), value, current)
            return current

        current = lax.fori_loop(0, (many + STEP - 1) // STEP, some, current)
        first = first + many * wide
    put(lax.shift_right_logical(first, 7), current)


def deal(turns, amplitudes, occ_count, virt_count, target):
    return pl.pallas_call(
        deal_kernel,
        in_specs=[scalars()] * 3 + [pl.BlockSpec(memory_space=pl.ANY)],
        out_specs=pl.BlockSpec(memory_space=pltpu.VMEM),
        out_shape=jax.ShapeDtypeStruct((ROWS, 6, turns, 8, VCAP), BF),
        scratch_shapes=[pltpu.VMEM((6, KO, 8, VCAP), BF), pltpu.SemaphoreType.DMA((IRREPS,))],
        compiler_params=pltpu.CompilerParams(vmem_limit_bytes=56 << 20),
        name="deal",
    )(occ_count, virt_count, target, amplitudes)


def repack_kernel(where, occ, virt, target, t_ref, out_ref):
    first_k = where[1] * 6
    irrep = first_k // OCAP
    k_base = first_k - irrep * OCAP
    n_occ = occ[irrep]
    n_virt = columns_of(occ, virt, target, irrep)
    c = lax.broadcasted_iota(jnp.int32, (VCAP, VCAP), 0)
    for turn in range(t_ref.shape[1]):
        held = t_ref[:, turn].astype(F32).reshape(ROWS, 6, 8, VCAP)
        for k in range(6):
            limit = jnp.where(k_base + k < n_occ, n_virt, 0)
            value = jnp.where(c < limit, held[:, k].reshape(VCAP, VCAP), 0.0)
            out_ref[k * VCAP:(k + 1) * VCAP, turn * VCAP:(turn + 1) * VCAP] = value.astype(BF)


def repack(landed, where, occ_count, virt_count, target):
    return pl.pallas_call(
        repack_kernel,
        in_specs=[scalars()] * 4 + [pl.BlockSpec(memory_space=pltpu.VMEM)],
        out_specs=pl.BlockSpec(memory_space=pltpu.VMEM),
        out_shape=jax.ShapeDtypeStruct((6 * VCAP, SIZES[-1] * VCAP), BF),
        compiler_params=pltpu.CompilerParams(vmem_limit_bytes=24 << 20),
        name="repack",
    )(where, occ_count, virt_count, target, landed)


def product_kernel(w_ref, t_ref, out_ref, w_held, t_held, out_held, w_sem, t_sem, out_sem):
    tall = w_ref.shape[0] // 4
    width = t_held.shape[1]
    t_copy = pltpu.make_async_copy(t_ref.at[:, :width], t_held, t_sem)
    w_copies = [
        pltpu.make_async_copy(
            w_ref.at[x * tall:(x + 1) * tall], w_held.at[x * tall:(x + 1) * tall], w_sem.at[x]
        )
        for x in range(4)
    ]
    t_copy.start()
    w_copies[0].start()
    t_copy.wait()
    out_copies = []
    for x in range(4):
        w_copies[x].wait()
        if x < 3:
            w_copies[x + 1].start()
        part = jnp.dot(
            w_held[x * tall:(x + 1) * tall, :], t_held[...], preferred_element_type=F32
        )
        for z in range(8):
            out_held[x, z] = part[z * BLOCK:(z + 1) * BLOCK].astype(BF)
        copy = pltpu.make_async_copy(out_held.at[x], out_ref.at[:, x], out_sem.at[x])
        copy.start()
        out_copies.append(copy)
    for copy in out_copies:
        copy.wait()


def product(turns, w_rows, t_rows):
    rows, depth = w_rows.shape
    width = turns * VCAP
    out = pl.pallas_call(
        product_kernel,
        in_specs=[pl.BlockSpec(memory_space=pl.ANY)] * 2,
        out_specs=pl.BlockSpec(memory_space=pl.ANY),
        out_shape=jax.ShapeDtypeStruct((8, 4, BLOCK, width), BF),
        scratch_shapes=[
            pltpu.VMEM((rows, depth), BF),
            pltpu.VMEM((depth, width), BF),
            pltpu.VMEM((4, 8, BLOCK, width), BF),
            pltpu.SemaphoreType.DMA((4,)),
            pltpu.SemaphoreType.DMA,
            pltpu.SemaphoreType.DMA((4,)),
        ],
        compiler_params=pltpu.CompilerParams(vmem_limit_bytes=56 << 20),
        name="product",
    )(w_rows, t_rows)
    return out.reshape(rows, width)


def send_kernel(where, occ, virt, target, parts_ref, out_ref, total):
    turns = total.shape[0]
    for turn in range(turns):
        at = turn * VCAP
        added = parts_ref[0, :, at:at + VCAP].astype(F32)
        for x in range(1, 4):
            added = added + parts_ref[x, :, at:at + VCAP].astype(F32)
        total[turn] = added.astype(BF)
    mine = where[0]
    first = jnp.int32(0)
    for h in range(IRREPS):
        wide = columns_of(occ, virt, target, h)
        for e in range(2):
            begin = lax.shift_right_logical(first + 12 * e * wide, 7)
            p = begin + jnp.bitwise_and(mine - begin + 16 * ROWS, 15)
            out_ref[2 * h + e] = total[jnp.minimum(lax.shift_right_logical(p, 4), turns - 1)]
        first = first + occ[h] * wide


def send_out(parts, where, occ_count, virt_count, target):
    return pl.pallas_call(
        send_kernel,
        in_specs=[scalars()] * 4 + [pl.BlockSpec(memory_space=pltpu.VMEM)],
        out_specs=pl.BlockSpec(memory_space=pltpu.VMEM),
        out_shape=jax.ShapeDtypeStruct((ROWS, BLOCK, VCAP), BF),
        scratch_shapes=[pltpu.VMEM((parts.shape[2] // VCAP, BLOCK, VCAP), BF)],
        compiler_params=pltpu.CompilerParams(vmem_limit_bytes=24 << 20),
        name="send_out",
    )(where, occ_count, virt_count, target, parts)


def place_kernel(where, occ, virt, target, got_ref, out_ref):
    row, col = where[0], where[1]
    irrep, half = row // 2, row % 2
    first = first_column(occ, virt, target, irrep)
    wide = columns_of(occ, virt, target, irrep)
    line = col * BLOCK + lax.broadcasted_iota(jnp.int32, (BLOCK, VCAP), 0)
    b = lax.broadcasted_iota(jnp.int32, (BLOCK, VCAP), 1)
    inside = (line // VCAP < occ[0]) & (line % VCAP < virt[target[0]]) & (b < wide)
    for l in range(12):
        s = half * 12 + l
        at = first + s * wide
        p = lax.shift_right_logical(at, 7)
        shift = jnp.bitwise_and(at, 127)
        here = got_ref[jnp.bitwise_and(p, 15)].astype(F32)
        after = got_ref[jnp.bitwise_and(p + 1, 15)].astype(F32)
        block = jnp.where(b >= shift, here, after)
        block = pltpu.roll(block, jnp.bitwise_and(VCAP - shift, 127), 1)
        keep = inside & (s < occ[irrep])
        out_ref[:, l * VCAP:(l + 1) * VCAP] = jnp.where(keep, block, 0.0).astype(BF)


def place(got, where, occ_count, virt_count, target):
    return pl.pallas_call(
        place_kernel,
        in_specs=[scalars()] * 4 + [pl.BlockSpec(memory_space=pltpu.VMEM)],
        out_specs=pl.BlockSpec(memory_space=pltpu.VMEM),
        out_shape=jax.ShapeDtypeStruct((BLOCK, 12 * VCAP), BF),
        compiler_params=pltpu.CompilerParams(vmem_limit_bytes=24 << 20),
        name="place",
    )(where, occ_count, virt_count, target, got)


def bring(turns, where, amplitudes, occ_count, virt_count, target):
    dealt = deal(turns, amplitudes, occ_count, virt_count, target)
    landed = lax.all_to_all(dealt, ("y", "core"), 0, 0, tiled=True)
    landed = landed.reshape(ROWS * 6, turns, 8, VCAP)
    return repack(landed, where, occ_count, virt_count, target)


def contract(turns, w_rows, t_rows, where, occ_count, virt_count, target):
    partial = product(turns, w_rows, t_rows)
    by_z = lax.psum_scatter(partial, "z", scatter_dimension=0, tiled=True)
    by_x = lax.all_to_all(by_z, "x", 0, 0, tiled=True).reshape(4, BLOCK, turns * VCAP)
    out = send_out(by_x, where, occ_count, virt_count, target)
    return lax.all_to_all(out, ("y", "core"), 0, 0, tiled=True)


def per_device(w_cycle, amplitudes, occ_count, virt_count, target):
    row = lax.axis_index("y") * 2 + lax.axis_index("core")
    col = lax.axis_index("x") * 8 + lax.axis_index("z")
    where = jnp.stack([row, col]).astype(jnp.int32)
    irreps = jnp.arange(IRREPS, dtype=jnp.int32)
    meets = jnp.bitwise_xor(irreps, target)[:, None] == irreps[None, :]
    pairs = jnp.sum(jnp.where(meets, occ_count[:, None] * virt_count[None, :], 0))
    case = sum((pairs > (ROWS * turns - 1) * VCAP).astype(jnp.int32) for turns in SIZES[:-1])
    counts = (occ_count, virt_count, target)
    w_rows = lax.all_gather(w_cycle, ("y", "core"), axis=0, tiled=True)
    t_rows = lax.switch(
        case, [functools.partial(bring, turns) for turns in SIZES], where, amplitudes, *counts
    )
    got = lax.switch(
        case, [functools.partial(contract, turns) for turns in SIZES],
        w_rows, t_rows, where, *counts,
    )
    return place(got, where, occ_count, virt_count, target)


def solution(mesh):
    chips = Mesh(mesh.devices.reshape(8, 2, 4, 8), ("y", "core", "x", "z"))
    row, col = ("y", "core"), ("x", "z")
    placed = (P(row, col), P(col, None, row, None), P(), P(), P())
    return jax.shard_map(
        per_device, mesh=chips, in_specs=placed, out_specs=P(col, row), check_vma=False
    )
```

```python
import functools

import jax
import jax.numpy as jnp
from jax import lax
from jax.experimental import pallas as pl
from jax.experimental.pallas import tpu as pltpu
from jax.sharding import Mesh, PartitionSpec as P

IRREPS = 8
OCAP = 24
VCAP = 128
KO = 192
ROWS = 16
SIZES = (5, 6, 8)
STEP = 12
BLOCK = 48
BF = jnp.bfloat16
F32 = jnp.float32


def scalars():
    return pl.BlockSpec(memory_space=pltpu.SMEM)


def columns_of(occ, virt, target, irrep):
    return virt[jnp.bitwise_xor(irrep, target[0])]


def first_column(occ, virt, target, irrep):
    total = jnp.int32(0)
    for h in range(IRREPS):
        total = total + jnp.where(h < irrep, occ[h] * columns_of(occ, virt, target, h), 0)
    return total


def size_class(pairs):
    return sum((pairs > (ROWS * turns - 1) * VCAP).astype(jnp.int32) for turns in SIZES[:-1])


def deal_kernel(occ, virt, target, t_ref, *rest):
    results, (held, packed, sem, out_sem) = rest[:len(SIZES)], rest[len(SIZES):]
    copies = [
        pltpu.make_async_copy(
            t_ref.at[:, h * OCAP:(h + 1) * OCAP], held.at[:, h * OCAP:(h + 1) * OCAP], sem.at[h]
        )
        for h in range(IRREPS)
    ]
    for copy in copies:
        copy.start()
    lane = lax.broadcasted_iota(jnp.int32, (48, VCAP), 1)

    def put(p, value):
        packed[jnp.bitwise_and(p, 15), :, lax.shift_right_logical(p, 4)] = (
            value.astype(BF).reshape(6, 8, VCAP)
        )

    current = jnp.zeros((48, VCAP), F32)
    first = jnp.int32(0)
    for h in range(IRREPS):
        copies[h].wait()
        many = occ[h]
        wide = columns_of(occ, virt, target, h)

        def some(g, current, h=h, first=first, many=many, wide=wide):
            for u in range(STEP):
                s = g * STEP + u
                at = first + jnp.minimum(s, many) * wide
                shift = jnp.bitwise_and(at, 127)
                value = held[:, h * OCAP + s].astype(F32).reshape(48, VCAP)
                value = pltpu.roll(value, shift, 1)
                current = jnp.where(lane >= shift, value, current)
                put(lax.shift_right_logical(at, 7), current)
                current = jnp.where((s < many) & (shift + wide >= VCAP), value, current)
            return current

        current = lax.fori_loop(0, (many + STEP - 1) // STEP, some, current)
        first = first + many * wide
    put(lax.shift_right_logical(first, 7), current)
    which = size_class(first)
    for n, turns in enumerate(SIZES):
        @pl.when(which == n)
        def _(n=n, turns=turns):
            copy = pltpu.make_async_copy(packed.at[:, :, :turns], results[n], out_sem)
            copy.start()
            copy.wait()


def deal(amplitudes, occ_count, virt_count, target):
    return pl.pallas_call(
        deal_kernel,
        in_specs=[scalars()] * 3 + [pl.BlockSpec(memory_space=pl.ANY)],
        out_specs=[pl.BlockSpec(memory_space=pl.ANY)] * len(SIZES),
        out_shape=[jax.ShapeDtypeStruct((ROWS, 6, turns, 8, VCAP), BF) for turns in SIZES],
        scratch_shapes=[
            pltpu.VMEM((6, KO, 8, VCAP), BF),
            pltpu.VMEM((ROWS, 6, SIZES[-1], 8, VCAP), BF),
            pltpu.SemaphoreType.DMA((IRREPS,)),
            pltpu.SemaphoreType.DMA,
        ],
        compiler_params=pltpu.CompilerParams(vmem_limit_bytes=56 << 20),
        name="deal",
    )(occ_count, virt_count, target, amplitudes)


def repack_kernel(where, occ, virt, target, t_ref, out_ref):
    first_k = where[1] * 6
    irrep = first_k // OCAP
    k_base = first_k - irrep * OCAP
    n_occ = occ[irrep]
    n_virt = columns_of(occ, virt, target, irrep)
    c = lax.broadcasted_iota(jnp.int32, (VCAP, VCAP), 0)
    for turn in range(t_ref.shape[1]):
        held = t_ref[:, turn].astype(F32).reshape(ROWS, 6, 8, VCAP)
        for k in range(6):
            limit = jnp.where(k_base + k < n_occ, n_virt, 0)
            value = jnp.where(c < limit, held[:, k].reshape(VCAP, VCAP), 0.0)
            out_ref[k * VCAP:(k + 1) * VCAP, turn * VCAP:(turn + 1) * VCAP] = value.astype(BF)


def repack(landed, where, occ_count, virt_count, target):
    turns = landed.shape[1]
    return pl.pallas_call(
        repack_kernel,
        in_specs=[scalars()] * 4 + [pl.BlockSpec(memory_space=pltpu.VMEM)],
        out_specs=pl.BlockSpec(memory_space=pltpu.VMEM),
        out_shape=jax.ShapeDtypeStruct((6 * VCAP, turns * VCAP), BF),
        compiler_params=pltpu.CompilerParams(vmem_limit_bytes=24 << 20),
        name="repack",
    )(where, occ_count, virt_count, target, landed)


def product_kernel(w_ref, t_ref, out_ref, held, sem):
    tall = 4 * BLOCK
    copies = []
    for n in range(8):
        value = jnp.dot(
            w_ref[n * tall:(n + 1) * tall, :], t_ref[...], preferred_element_type=F32
        )
        for z in range(4):
            held[n, z] = value[z * BLOCK:(z + 1) * BLOCK].astype(BF)
        begin = 4 * (n % 2)
        copy = pltpu.make_async_copy(held.at[n], out_ref.at[begin:begin + 4, n // 2], sem.at[n])
        copy.start()
        copies.append(copy)
    for copy in copies:
        copy.wait()


def product(w_rows, t_rows):
    rows = w_rows.shape[0]
    width = t_rows.shape[1]
    out = pl.pallas_call(
        product_kernel,
        in_specs=[pl.BlockSpec(memory_space=pltpu.VMEM)] * 2,
        out_specs=pl.BlockSpec(memory_space=pl.ANY),
        out_shape=jax.ShapeDtypeStruct((8, 4, BLOCK, width), BF),
        scratch_shapes=[pltpu.VMEM((8, 4, BLOCK, width), BF), pltpu.SemaphoreType.DMA((8,))],
        compiler_params=pltpu.CompilerParams(vmem_limit_bytes=24 << 20),
        name="product",
    )(w_rows, t_rows)
    return out.reshape(rows, width)


def send_kernel(where, occ, virt, target, parts_ref, out_ref, total):
    turns = total.shape[0]
    for turn in range(turns):
        at = turn * VCAP
        added = parts_ref[0, :, at:at + VCAP].astype(F32)
        for x in range(1, 4):
            added = added + parts_ref[x, :, at:at + VCAP].astype(F32)
        total[turn] = added.astype(BF)
    mine = where[0]
    first = jnp.int32(0)
    for h in range(IRREPS):
        wide = columns_of(occ, virt, target, h)
        for e in range(2):
            begin = lax.shift_right_logical(first + 12 * e * wide, 7)
            p = begin + jnp.bitwise_and(mine - begin + 16 * ROWS, 15)
            out_ref[2 * h + e] = total[jnp.minimum(lax.shift_right_logical(p, 4), turns - 1)]
        first = first + occ[h] * wide


def send_out(parts, where, occ_count, virt_count, target):
    return pl.pallas_call(
        send_kernel,
        in_specs=[scalars()] * 4 + [pl.BlockSpec(memory_space=pltpu.VMEM)],
        out_specs=pl.BlockSpec(memory_space=pltpu.VMEM),
        out_shape=jax.ShapeDtypeStruct((ROWS, BLOCK, VCAP), BF),
        scratch_shapes=[pltpu.VMEM((parts.shape[2] // VCAP, BLOCK, VCAP), BF)],
        compiler_params=pltpu.CompilerParams(vmem_limit_bytes=24 << 20),
        name="send_out",
    )(where, occ_count, virt_count, target, parts)


def place_kernel(where, occ, virt, target, got_ref, out_ref):
    row, col = where[0], where[1]
    irrep, half = row // 2, row % 2
    first = first_column(occ, virt, target, irrep)
    wide = columns_of(occ, virt, target, irrep)
    line = col * BLOCK + lax.broadcasted_iota(jnp.int32, (BLOCK, VCAP), 0)
    b = lax.broadcasted_iota(jnp.int32, (BLOCK, VCAP), 1)
    inside = (line // VCAP < occ[0]) & (line % VCAP < virt[target[0]]) & (b < wide)
    for l in range(12):
        s = half * 12 + l
        at = first + s * wide
        p = lax.shift_right_logical(at, 7)
        shift = jnp.bitwise_and(at, 127)
        here = got_ref[jnp.bitwise_and(p, 15)].astype(F32)
        after = got_ref[jnp.bitwise_and(p + 1, 15)].astype(F32)
        block = jnp.where(b >= shift, here, after)
        block = pltpu.roll(block, jnp.bitwise_and(VCAP - shift, 127), 1)
        keep = inside & (s < occ[irrep])
        out_ref[:, l * VCAP:(l + 1) * VCAP] = jnp.where(keep, block, 0.0).astype(BF)


def place(got, where, occ_count, virt_count, target):
    return pl.pallas_call(
        place_kernel,
        in_specs=[scalars()] * 4 + [pl.BlockSpec(memory_space=pltpu.VMEM)],
        out_specs=pl.BlockSpec(memory_space=pltpu.VMEM),
        out_shape=jax.ShapeDtypeStruct((BLOCK, 12 * VCAP), BF),
        compiler_params=pltpu.CompilerParams(vmem_limit_bytes=32 << 20),
        name="place",
    )(where, occ_count, virt_count, target, got)


def contract(turns, w_cycle, dealt, *masks):
    line = ("y", "core")
    w_rows = lax.all_gather(w_cycle, line, axis=0, tiled=True)
    landed = lax.all_to_all(dealt[SIZES.index(turns)], line, 0, 0, tiled=True)
    t_rows = repack(landed.reshape(ROWS * 6, turns, 8, VCAP), *masks)
    partial = product(w_rows, t_rows)
    by_z = lax.psum_scatter(partial, "z", scatter_dimension=0, tiled=True)
    by_x = lax.all_to_all(by_z, "x", 0, 0, tiled=True).reshape(4, BLOCK, turns * VCAP)
    return lax.all_to_all(send_out(by_x, *masks), line, 0, 0, tiled=True)


def per_device(w_cycle, amplitudes, occ_count, virt_count, target):
    row = lax.axis_index("y") * 2 + lax.axis_index("core")
    col = lax.axis_index("x") * 8 + lax.axis_index("z")
    masks = (jnp.stack([row, col]).astype(jnp.int32), occ_count, virt_count, target)
    irreps = jnp.arange(IRREPS, dtype=jnp.int32)
    meets = jnp.bitwise_xor(irreps, target)[:, None] == irreps[None, :]
    pairs = jnp.sum(jnp.where(meets, occ_count[:, None] * virt_count[None, :], 0))
    dealt = deal(amplitudes, occ_count, virt_count, target)
    got = lax.switch(
        size_class(pairs),
        [functools.partial(contract, turns) for turns in SIZES],
        w_cycle, dealt, *masks,
    )
    return place(got, *masks)


def solution(mesh):
    chips = Mesh(mesh.devices.reshape(8, 2, 4, 8), ("y", "core", "x", "z"))
    row, col = ("y", "core"), ("x", "z")
    placed = (P(row, col), P(col, None, row, None), P(), P(), P())
    return jax.shard_map(
        per_device, mesh=chips, in_specs=placed, out_specs=P(col, row), check_vma=False
    )
```

```python
import functools

import jax
import jax.numpy as jnp
from jax import lax
from jax.experimental import pallas as pl
from jax.experimental.pallas import tpu as pltpu
from jax.sharding import Mesh, PartitionSpec as P

IRREPS = 8
OCAP = 24
VCAP = 128
KO = 192
ROWS = 16
SIZES = (5, 6, 8)
STEP = 12
BLOCK = 48
BF = jnp.bfloat16
F32 = jnp.float32


def scalars():
    return pl.BlockSpec(memory_space=pltpu.SMEM)


def columns_of(occ, virt, target, irrep):
    return virt[jnp.bitwise_xor(irrep, target[0])]


def first_column(occ, virt, target, irrep):
    total = jnp.int32(0)
    for h in range(IRREPS):
        total = total + jnp.where(h < irrep, occ[h] * columns_of(occ, virt, target, h), 0)
    return total


def deal_kernel(occ, virt, target, t_ref, out_ref, held, sem):
    copies = [
        pltpu.make_async_copy(
            t_ref.at[:, h * OCAP:(h + 1) * OCAP], held.at[:, h * OCAP:(h + 1) * OCAP], sem.at[h]
        )
        for h in range(IRREPS)
    ]
    for copy in copies:
        copy.start()
    lane = lax.broadcasted_iota(jnp.int32, (48, VCAP), 1)

    def put(p, value):
        out_ref[jnp.bitwise_and(p, 15), :, lax.shift_right_logical(p, 4)] = (
            value.astype(BF).reshape(6, 8, VCAP)
        )

    current = jnp.zeros((48, VCAP), F32)
    first = jnp.int32(0)
    for h in range(IRREPS):
        copies[h].wait()
        many = occ[h]
        wide = columns_of(occ, virt, target, h)

        def some(g, current, h=h, first=first, many=many, wide=wide):
            for u in range(STEP):
                s = g * STEP + u
                at = first + jnp.minimum(s, many) * wide
                shift = jnp.bitwise_and(at, 127)
                value = held[:, h * OCAP + s].astype(F32).reshape(48, VCAP)
                value = pltpu.roll(value, shift, 1)
                current = jnp.where(lane >= shift, value, current)
                put(lax.shift_right_logical(at, 7), current)
                current = jnp.where((s < many) & (shift + wide >= VCAP), value, current)
            return current

        current = lax.fori_loop(0, (many + STEP - 1) // STEP, some, current)
        first = first + many * wide
    put(lax.shift_right_logical(first, 7), current)


def deal(turns, amplitudes, occ_count, virt_count, target):
    return pl.pallas_call(
        deal_kernel,
        in_specs=[scalars()] * 3 + [pl.BlockSpec(memory_space=pl.ANY)],
        out_specs=pl.BlockSpec(memory_space=pltpu.VMEM),
        out_shape=jax.ShapeDtypeStruct((ROWS, 6, turns, 8, VCAP), BF),
        scratch_shapes=[pltpu.VMEM((6, KO, 8, VCAP), BF), pltpu.SemaphoreType.DMA((IRREPS,))],
        compiler_params=pltpu.CompilerParams(vmem_limit_bytes=56 << 20),
        name="deal",
    )(occ_count, virt_count, target, amplitudes)


def repack_kernel(where, occ, virt, target, t_ref, out_ref):
    first_k = where[1] * 6
    irrep = first_k // OCAP
    k_base = first_k - irrep * OCAP
    n_occ = occ[irrep]
    n_virt = columns_of(occ, virt, target, irrep)
    c = lax.broadcasted_iota(jnp.int32, (VCAP, VCAP), 0)
    for turn in range(t_ref.shape[1]):
        held = t_ref[:, turn].astype(F32).reshape(ROWS, 6, 8, VCAP)
        for k in range(6):
            limit = jnp.where(k_base + k < n_occ, n_virt, 0)
            value = jnp.where(c < limit, held[:, k].reshape(VCAP, VCAP), 0.0)
            out_ref[k * VCAP:(k + 1) * VCAP, turn * VCAP:(turn + 1) * VCAP] = value.astype(BF)


def repack(landed, where, occ_count, virt_count, target):
    turns = landed.shape[1]
    return pl.pallas_call(
        repack_kernel,
        in_specs=[scalars()] * 4 + [pl.BlockSpec(memory_space=pltpu.VMEM)],
        out_specs=pl.BlockSpec(memory_space=pltpu.VMEM),
        out_shape=jax.ShapeDtypeStruct((6 * VCAP, turns * VCAP), BF),
        compiler_params=pltpu.CompilerParams(vmem_limit_bytes=24 << 20),
        name="repack",
    )(where, occ_count, virt_count, target, landed)


def product_kernel(w_ref, t_ref, out_ref, held, sem):
    tall = 4 * BLOCK
    copies = []
    for n in range(8):
        value = jnp.dot(
            w_ref[n * tall:(n + 1) * tall, :], t_ref[...], preferred_element_type=F32
        )
        for z in range(4):
            held[n, z] = value[z * BLOCK:(z + 1) * BLOCK].astype(BF)
        begin = 4 * (n % 2)
        copy = pltpu.make_async_copy(held.at[n], out_ref.at[begin:begin + 4, n // 2], sem.at[n])
        copy.start()
        copies.append(copy)
    for copy in copies:
        copy.wait()


def product(w_rows, t_rows):
    rows = w_rows.shape[0]
    width = t_rows.shape[1]
    out = pl.pallas_call(
        product_kernel,
        in_specs=[pl.BlockSpec(memory_space=pltpu.VMEM)] * 2,
        out_specs=pl.BlockSpec(memory_space=pl.ANY),
        out_shape=jax.ShapeDtypeStruct((8, 4, BLOCK, width), BF),
        scratch_shapes=[pltpu.VMEM((8, 4, BLOCK, width), BF), pltpu.SemaphoreType.DMA((8,))],
        compiler_params=pltpu.CompilerParams(vmem_limit_bytes=24 << 20),
        name="product",
    )(w_rows, t_rows)
    return out.reshape(rows, width)


def send_kernel(where, occ, virt, target, parts_ref, out_ref, total):
    turns = total.shape[0]
    for turn in range(turns):
        at = turn * VCAP
        added = parts_ref[0, :, at:at + VCAP].astype(F32)
        for x in range(1, 4):
            added = added + parts_ref[x, :, at:at + VCAP].astype(F32)
        total[turn] = added.astype(BF)
    mine = where[0]
    first = jnp.int32(0)
    for h in range(IRREPS):
        wide = columns_of(occ, virt, target, h)
        for e in range(2):
            begin = lax.shift_right_logical(first + 12 * e * wide, 7)
            p = begin + jnp.bitwise_and(mine - begin + 16 * ROWS, 15)
            out_ref[2 * h + e] = total[jnp.minimum(lax.shift_right_logical(p, 4), turns - 1)]
        first = first + occ[h] * wide


def send_out(parts, where, occ_count, virt_count, target):
    return pl.pallas_call(
        send_kernel,
        in_specs=[scalars()] * 4 + [pl.BlockSpec(memory_space=pltpu.VMEM)],
        out_specs=pl.BlockSpec(memory_space=pltpu.VMEM),
        out_shape=jax.ShapeDtypeStruct((ROWS, BLOCK, VCAP), BF),
        scratch_shapes=[pltpu.VMEM((parts.shape[2] // VCAP, BLOCK, VCAP), BF)],
        compiler_params=pltpu.CompilerParams(vmem_limit_bytes=24 << 20),
        name="send_out",
    )(where, occ_count, virt_count, target, parts)


def place_kernel(where, occ, virt, target, got_ref, out_ref):
    row, col = where[0], where[1]
    irrep, half = row // 2, row % 2
    first = first_column(occ, virt, target, irrep)
    wide = columns_of(occ, virt, target, irrep)
    line = col * BLOCK + lax.broadcasted_iota(jnp.int32, (BLOCK, VCAP), 0)
    b = lax.broadcasted_iota(jnp.int32, (BLOCK, VCAP), 1)
    inside = (line // VCAP < occ[0]) & (line % VCAP < virt[target[0]]) & (b < wide)
    for l in range(12):
        s = half * 12 + l
        at = first + s * wide
        p = lax.shift_right_logical(at, 7)
        shift = jnp.bitwise_and(at, 127)
        here = got_ref[jnp.bitwise_and(p, 15)].astype(F32)
        after = got_ref[jnp.bitwise_and(p + 1, 15)].astype(F32)
        block = jnp.where(b >= shift, here, after)
        block = pltpu.roll(block, jnp.bitwise_and(VCAP - shift, 127), 1)
        keep = inside & (s < occ[irrep])
        out_ref[:, l * VCAP:(l + 1) * VCAP] = jnp.where(keep, block, 0.0).astype(BF)


def place(got, where, occ_count, virt_count, target):
    return pl.pallas_call(
        place_kernel,
        in_specs=[scalars()] * 4 + [pl.BlockSpec(memory_space=pltpu.VMEM)],
        out_specs=pl.BlockSpec(memory_space=pltpu.VMEM),
        out_shape=jax.ShapeDtypeStruct((BLOCK, 12 * VCAP), BF),
        compiler_params=pltpu.CompilerParams(vmem_limit_bytes=32 << 20),
        name="place",
    )(where, occ_count, virt_count, target, got)


def class_kernel(occ, virt, target, out):
    pairs = first_column(occ, virt, target, IRREPS)
    out[0] = sum((pairs > (ROWS * turns - 1) * VCAP).astype(jnp.int32) for turns in SIZES[:-1])


def size_class(occ_count, virt_count, target):
    return pl.pallas_call(
        class_kernel,
        in_specs=[scalars()] * 3,
        out_specs=scalars(),
        out_shape=jax.ShapeDtypeStruct((1,), jnp.int32),
        name="size_class",
    )(occ_count, virt_count, target)


def contract(turns, w_cycle, amplitudes, *masks):
    line = ("y", "core")
    w_rows = lax.all_gather(w_cycle, line, axis=0, tiled=True)
    landed = lax.all_to_all(deal(turns, amplitudes, *masks[1:]), line, 0, 0, tiled=True)
    t_rows = repack(landed.reshape(ROWS * 6, turns, 8, VCAP), *masks)
    partial = product(w_rows, t_rows)
    by_z = lax.psum_scatter(partial, "z", scatter_dimension=0, tiled=True)
    by_x = lax.all_to_all(by_z, "x", 0, 0, tiled=True).reshape(4, BLOCK, turns * VCAP)
    return lax.all_to_all(send_out(by_x, *masks), line, 0, 0, tiled=True)


def per_device(w_cycle, amplitudes, occ_count, virt_count, target):
    row = lax.axis_index("y") * 2 + lax.axis_index("core")
    col = lax.axis_index("x") * 8 + lax.axis_index("z")
    masks = (jnp.stack([row, col]).astype(jnp.int32), occ_count, virt_count, target)
    got = lax.switch(
        size_class(occ_count, virt_count, target)[0],
        [functools.partial(contract, turns) for turns in SIZES],
        w_cycle, amplitudes, *masks,
    )
    return place(got, *masks)


def solution(mesh):
    chips = Mesh(mesh.devices.reshape(8, 2, 4, 8), ("y", "core", "x", "z"))
    row, col = ("y", "core"), ("x", "z")
    placed = (P(row, col), P(col, None, row, None), P(), P(), P())
    return jax.shard_map(
        per_device, mesh=chips, in_specs=placed, out_specs=P(col, row), check_vma=False
    )
```

```python
import functools

import jax
import jax.numpy as jnp
from jax import lax
from jax.experimental import pallas as pl
from jax.experimental.pallas import tpu as pltpu
from jax.sharding import Mesh, PartitionSpec as P

IRREPS = 8
OCAP = 24
VCAP = 128
KO = 192
ROWS = 16
SIZES = (5, 6, 8)
STEP = 12
BLOCK = 48
BF = jnp.bfloat16
F32 = jnp.float32


def scalars():
    return pl.BlockSpec(memory_space=pltpu.SMEM)


def columns_of(occ, virt, target, irrep):
    return virt[jnp.bitwise_xor(irrep, target[0])]


def first_column(occ, virt, target, irrep):
    total = jnp.int32(0)
    for h in range(IRREPS):
        total = total + jnp.where(h < irrep, occ[h] * columns_of(occ, virt, target, h), 0)
    return total


def size_class(pairs):
    return sum((pairs > (ROWS * turns - 1) * VCAP).astype(jnp.int32) for turns in SIZES[:-1])


def deal_kernel(occ, virt, target, t_ref, *rest):
    results, (class_ref, held, packed, sem, out_sem) = rest[:len(SIZES)], rest[len(SIZES):]
    copies = [
        pltpu.make_async_copy(
            t_ref.at[:, h * OCAP:(h + 1) * OCAP], held.at[:, h * OCAP:(h + 1) * OCAP], sem.at[h]
        )
        for h in range(IRREPS)
    ]
    for copy in copies:
        copy.start()
    lane = lax.broadcasted_iota(jnp.int32, (48, VCAP), 1)

    def put(p, value):
        packed[jnp.bitwise_and(p, 15), :, lax.shift_right_logical(p, 4)] = (
            value.astype(BF).reshape(6, 8, VCAP)
        )

    current = jnp.zeros((48, VCAP), F32)
    first = jnp.int32(0)
    for h in range(IRREPS):
        copies[h].wait()
        many = occ[h]
        wide = columns_of(occ, virt, target, h)

        def some(g, current, h=h, first=first, many=many, wide=wide):
            for u in range(STEP):
                s = g * STEP + u
                at = first + jnp.minimum(s, many) * wide
                shift = jnp.bitwise_and(at, 127)
                value = held[:, h * OCAP + s].astype(F32).reshape(48, VCAP)
                value = pltpu.roll(value, shift, 1)
                current = jnp.where(lane >= shift, value, current)
                put(lax.shift_right_logical(at, 7), current)
                current = jnp.where((s < many) & (shift + wide >= VCAP), value, current)
            return current

        current = lax.fori_loop(0, (many + STEP - 1) // STEP, some, current)
        first = first + many * wide
    put(lax.shift_right_logical(first, 7), current)
    which = size_class(first)
    class_ref[0] = which
    for n, turns in enumerate(SIZES):
        @pl.when(which == n)
        def _(n=n, turns=turns):
            copy = pltpu.make_async_copy(packed.at[:, :, :turns], results[n], out_sem)
            copy.start()
            copy.wait()


def deal(amplitudes, occ_count, virt_count, target):
    return pl.pallas_call(
        deal_kernel,
        in_specs=[scalars()] * 3 + [pl.BlockSpec(memory_space=pl.ANY)],
        out_specs=[pl.BlockSpec(memory_space=pl.ANY)] * len(SIZES) + [scalars()],
        out_shape=[jax.ShapeDtypeStruct((ROWS, 6, turns, 8, VCAP), BF) for turns in SIZES]
        + [jax.ShapeDtypeStruct((1,), jnp.int32)],
        scratch_shapes=[
            pltpu.VMEM((6, KO, 8, VCAP), BF),
            pltpu.VMEM((ROWS, 6, SIZES[-1], 8, VCAP), BF),
            pltpu.SemaphoreType.DMA((IRREPS,)),
            pltpu.SemaphoreType.DMA,
        ],
        compiler_params=pltpu.CompilerParams(vmem_limit_bytes=56 << 20),
        name="deal",
    )(occ_count, virt_count, target, amplitudes)


def repack_kernel(where, occ, virt, target, t_ref, out_ref):
    first_k = where[1] * 6
    irrep = first_k // OCAP
    k_base = first_k - irrep * OCAP
    n_occ = occ[irrep]
    n_virt = columns_of(occ, virt, target, irrep)
    c = lax.broadcasted_iota(jnp.int32, (VCAP, VCAP), 0)
    for turn in range(t_ref.shape[1]):
        held = t_ref[:, turn].astype(F32).reshape(ROWS, 6, 8, VCAP)
        for k in range(6):
            limit = jnp.where(k_base + k < n_occ, n_virt, 0)
            value = jnp.where(c < limit, held[:, k].reshape(VCAP, VCAP), 0.0)
            out_ref[k * VCAP:(k + 1) * VCAP, turn * VCAP:(turn + 1) * VCAP] = value.astype(BF)


def repack(landed, where, occ_count, virt_count, target):
    turns = landed.shape[1]
    return pl.pallas_call(
        repack_kernel,
        in_specs=[scalars()] * 4 + [pl.BlockSpec(memory_space=pltpu.VMEM)],
        out_specs=pl.BlockSpec(memory_space=pltpu.VMEM),
        out_shape=jax.ShapeDtypeStruct((6 * VCAP, turns * VCAP), BF),
        compiler_params=pltpu.CompilerParams(vmem_limit_bytes=24 << 20),
        name="repack",
    )(where, occ_count, virt_count, target, landed)


def product_kernel(w_ref, t_ref, out_ref, held, sem):
    tall = 4 * BLOCK
    copies = []
    for n in range(8):
        value = jnp.dot(
            w_ref[n * tall:(n + 1) * tall, :], t_ref[...], preferred_element_type=F32
        )
        for z in range(4):
            held[n, z] = value[z * BLOCK:(z + 1) * BLOCK].astype(BF)
        begin = 4 * (n % 2)
        copy = pltpu.make_async_copy(held.at[n], out_ref.at[begin:begin + 4, n // 2], sem.at[n])
        copy.start()
        copies.append(copy)
    for copy in copies:
        copy.wait()


def product(w_rows, t_rows):
    rows = w_rows.shape[0]
    width = t_rows.shape[1]
    out = pl.pallas_call(
        product_kernel,
        in_specs=[pl.BlockSpec(memory_space=pltpu.VMEM)] * 2,
        out_specs=pl.BlockSpec(memory_space=pl.ANY),
        out_shape=jax.ShapeDtypeStruct((8, 4, BLOCK, width), BF),
        scratch_shapes=[pltpu.VMEM((8, 4, BLOCK, width), BF), pltpu.SemaphoreType.DMA((8,))],
        compiler_params=pltpu.CompilerParams(vmem_limit_bytes=24 << 20),
        name="product",
    )(w_rows, t_rows)
    return out.reshape(rows, width)


def send_kernel(where, occ, virt, target, parts_ref, out_ref, total):
    turns = total.shape[0]
    for turn in range(turns):
        at = turn * VCAP
        added = parts_ref[0, :, at:at + VCAP].astype(F32)
        for x in range(1, 4):
            added = added + parts_ref[x, :, at:at + VCAP].astype(F32)
        total[turn] = added.astype(BF)
    mine = where[0]
    first = jnp.int32(0)
    for h in range(IRREPS):
        wide = columns_of(occ, virt, target, h)
        for e in range(2):
            begin = lax.shift_right_logical(first + 12 * e * wide, 7)
            p = begin + jnp.bitwise_and(mine - begin + 16 * ROWS, 15)
            out_ref[2 * h + e] = total[jnp.minimum(lax.shift_right_logical(p, 4), turns - 1)]
        first = first + occ[h] * wide


def send_out(parts, where, occ_count, virt_count, target):
    return pl.pallas_call(
        send_kernel,
        in_specs=[scalars()] * 4 + [pl.BlockSpec(memory_space=pltpu.VMEM)],
        out_specs=pl.BlockSpec(memory_space=pltpu.VMEM),
        out_shape=jax.ShapeDtypeStruct((ROWS, BLOCK, VCAP), BF),
        scratch_shapes=[pltpu.VMEM((parts.shape[2] // VCAP, BLOCK, VCAP), BF)],
        compiler_params=pltpu.CompilerParams(vmem_limit_bytes=24 << 20),
        name="send_out",
    )(where, occ_count, virt_count, target, parts)


def place_kernel(where, occ, virt, target, got_ref, out_ref):
    row, col = where[0], where[1]
    irrep, half = row // 2, row % 2
    first = first_column(occ, virt, target, irrep)
    wide = columns_of(occ, virt, target, irrep)
    line = col * BLOCK + lax.broadcasted_iota(jnp.int32, (BLOCK, VCAP), 0)
    b = lax.broadcasted_iota(jnp.int32, (BLOCK, VCAP), 1)
    inside = (line // VCAP < occ[0]) & (line % VCAP < virt[target[0]]) & (b < wide)
    for l in range(12):
        s = half * 12 + l
        at = first + s * wide
        p = lax.shift_right_logical(at, 7)
        shift = jnp.bitwise_and(at, 127)
        here = got_ref[jnp.bitwise_and(p, 15)].astype(F32)
        after = got_ref[jnp.bitwise_and(p + 1, 15)].astype(F32)
        block = jnp.where(b >= shift, here, after)
        block = pltpu.roll(block, jnp.bitwise_and(VCAP - shift, 127), 1)
        keep = inside & (s < occ[irrep])
        out_ref[:, l * VCAP:(l + 1) * VCAP] = jnp.where(keep, block, 0.0).astype(BF)


def place(got, where, occ_count, virt_count, target):
    return pl.pallas_call(
        place_kernel,
        in_specs=[scalars()] * 4 + [pl.BlockSpec(memory_space=pltpu.VMEM)],
        out_specs=pl.BlockSpec(memory_space=pltpu.VMEM),
        out_shape=jax.ShapeDtypeStruct((BLOCK, 12 * VCAP), BF),
        compiler_params=pltpu.CompilerParams(vmem_limit_bytes=32 << 20),
        name="place",
    )(where, occ_count, virt_count, target, got)


def contract(turns, w_cycle, dealt, *masks):
    line = ("y", "core")
    w_rows = lax.all_gather(w_cycle, line, axis=0, tiled=True)
    landed = lax.all_to_all(dealt[SIZES.index(turns)], line, 0, 0, tiled=True)
    t_rows = repack(landed.reshape(ROWS * 6, turns, 8, VCAP), *masks)
    partial = product(w_rows, t_rows)
    by_z = lax.psum_scatter(partial, "z", scatter_dimension=0, tiled=True)
    by_x = lax.all_to_all(by_z, "x", 0, 0, tiled=True).reshape(4, BLOCK, turns * VCAP)
    return lax.all_to_all(send_out(by_x, *masks), line, 0, 0, tiled=True)


def per_device(w_cycle, amplitudes, occ_count, virt_count, target):
    row = lax.axis_index("y") * 2 + lax.axis_index("core")
    col = lax.axis_index("x") * 8 + lax.axis_index("z")
    masks = (jnp.stack([row, col]).astype(jnp.int32), occ_count, virt_count, target)
    *dealt, which = deal(amplitudes, occ_count, virt_count, target)
    got = lax.switch(
        which[0],
        [functools.partial(contract, turns) for turns in SIZES],
        w_cycle, dealt, *masks,
    )
    return place(got, *masks)


def solution(mesh):
    chips = Mesh(mesh.devices.reshape(8, 2, 4, 8), ("y", "core", "x", "z"))
    row, col = ("y", "core"), ("x", "z")
    placed = (P(row, col), P(col, None, row, None), P(), P(), P())
    return jax.shard_map(
        per_device, mesh=chips, in_specs=placed, out_specs=P(col, row), check_vma=False
    )
```

```python
import functools

import jax
import jax.numpy as jnp
from jax import lax
from jax.experimental import pallas as pl
from jax.experimental.pallas import tpu as pltpu
from jax.sharding import Mesh, PartitionSpec as P

IRREPS = 8
OCAP = 24
VCAP = 128
KO = 192
ROWS = 16
SIZES = (5, 6, 8)
STEP = 12
BLOCK = 48
BF = jnp.bfloat16
F32 = jnp.float32


def scalars():
    return pl.BlockSpec(memory_space=pltpu.SMEM)


def columns_of(occ, virt, target, irrep):
    return virt[jnp.bitwise_xor(irrep, target[0])]


def first_column(occ, virt, target, irrep):
    total = jnp.int32(0)
    for h in range(IRREPS):
        total = total + jnp.where(h < irrep, occ[h] * columns_of(occ, virt, target, h), 0)
    return total


def size_class(pairs):
    return sum((pairs > (ROWS * turns - 1) * VCAP).astype(jnp.int32) for turns in SIZES[:-1])


def deal_kernel(occ, virt, target, t_ref, *rest):
    results, (class_ref, held, packed, sem, out_sem) = rest[:len(SIZES)], rest[len(SIZES):]
    copies = [
        pltpu.make_async_copy(
            t_ref.at[:, h * OCAP:(h + 1) * OCAP], held.at[:, h * OCAP:(h + 1) * OCAP], sem.at[h]
        )
        for h in range(IRREPS)
    ]
    for copy in copies:
        copy.start()
    lane = lax.broadcasted_iota(jnp.int32, (48, VCAP), 1)

    def put(p, value):
        packed[jnp.bitwise_and(p, 15), :, lax.shift_right_logical(p, 4)] = (
            value.astype(BF).reshape(6, 8, VCAP)
        )

    current = jnp.zeros((48, VCAP), F32)
    first = jnp.int32(0)
    for h in range(IRREPS):
        copies[h].wait()
        many = occ[h]
        wide = columns_of(occ, virt, target, h)

        def some(g, current, h=h, first=first, many=many, wide=wide):
            for u in range(STEP):
                s = g * STEP + u
                at = first + jnp.minimum(s, many) * wide
                shift = jnp.bitwise_and(at, 127)
                value = held[:, h * OCAP + s].astype(F32).reshape(48, VCAP)
                value = pltpu.roll(value, shift, 1)
                current = jnp.where(lane >= shift, value, current)
                put(lax.shift_right_logical(at, 7), current)
                current = jnp.where((s < many) & (shift + wide >= VCAP), value, current)
            return current

        current = lax.fori_loop(0, (many + STEP - 1) // STEP, some, current)
        first = first + many * wide
    put(lax.shift_right_logical(first, 7), current)
    which = size_class(first)
    class_ref[0] = which
    for n, turns in enumerate(SIZES):
        @pl.when(which == n)
        def _(n=n, turns=turns):
            copy = pltpu.make_async_copy(packed.at[:, :, :turns], results[n], out_sem)
            copy.start()
            copy.wait()


def deal(amplitudes, occ_count, virt_count, target):
    return pl.pallas_call(
        deal_kernel,
        in_specs=[scalars()] * 3 + [pl.BlockSpec(memory_space=pl.ANY)],
        out_specs=[pl.BlockSpec(memory_space=pl.ANY)] * len(SIZES) + [scalars()],
        out_shape=[jax.ShapeDtypeStruct((ROWS, 6, turns, 8, VCAP), BF) for turns in SIZES]
        + [jax.ShapeDtypeStruct((1,), jnp.int32)],
        scratch_shapes=[
            pltpu.VMEM((6, KO, 8, VCAP), BF),
            pltpu.VMEM((ROWS, 6, SIZES[-1], 8, VCAP), BF),
            pltpu.SemaphoreType.DMA((IRREPS,)),
            pltpu.SemaphoreType.DMA,
        ],
        compiler_params=pltpu.CompilerParams(vmem_limit_bytes=56 << 20),
        name="deal",
    )(occ_count, virt_count, target, amplitudes)


def repack_kernel(where, occ, virt, target, t_ref, out_ref):
    first_k = where[1] * 6
    irrep = first_k // OCAP
    k_base = first_k - irrep * OCAP
    n_occ = occ[irrep]
    n_virt = columns_of(occ, virt, target, irrep)
    c = lax.broadcasted_iota(jnp.int32, (VCAP, VCAP), 0)
    for turn in range(t_ref.shape[1]):
        held = t_ref[:, turn].astype(F32).reshape(ROWS, 6, 8, VCAP)
        for k in range(6):
            limit = jnp.where(k_base + k < n_occ, n_virt, 0)
            value = jnp.where(c < limit, held[:, k].reshape(VCAP, VCAP), 0.0)
            out_ref[k * VCAP:(k + 1) * VCAP, turn * VCAP:(turn + 1) * VCAP] = value.astype(BF)


def repack(landed, where, occ_count, virt_count, target):
    return pl.pallas_call(
        repack_kernel,
        in_specs=[scalars()] * 4 + [pl.BlockSpec(memory_space=pltpu.VMEM)],
        out_specs=pl.BlockSpec(memory_space=pltpu.VMEM),
        out_shape=jax.ShapeDtypeStruct((6 * VCAP, SIZES[-1] * VCAP), BF),
        compiler_params=pltpu.CompilerParams(vmem_limit_bytes=24 << 20),
        name="repack",
    )(where, occ_count, virt_count, target, landed)


def product_kernel(w_ref, t_ref, out_ref, held, sem):
    tall, width = 4 * BLOCK, held.shape[3]
    copies = []
    for n in range(8):
        value = jnp.dot(
            w_ref[n * tall:(n + 1) * tall, :], t_ref[:, :width], preferred_element_type=F32
        )
        for z in range(4):
            held[n, z] = value[z * BLOCK:(z + 1) * BLOCK].astype(BF)
        begin = 4 * (n % 2)
        copy = pltpu.make_async_copy(held.at[n], out_ref.at[begin:begin + 4, n // 2], sem.at[n])
        copy.start()
        copies.append(copy)
    for copy in copies:
        copy.wait()


def product(turns, w_rows, t_rows):
    rows = w_rows.shape[0]
    width = turns * VCAP
    out = pl.pallas_call(
        product_kernel,
        in_specs=[pl.BlockSpec(memory_space=pltpu.VMEM)] * 2,
        out_specs=pl.BlockSpec(memory_space=pl.ANY),
        out_shape=jax.ShapeDtypeStruct((8, 4, BLOCK, width), BF),
        scratch_shapes=[pltpu.VMEM((8, 4, BLOCK, width), BF), pltpu.SemaphoreType.DMA((8,))],
        compiler_params=pltpu.CompilerParams(vmem_limit_bytes=24 << 20),
        name="product",
    )(w_rows, t_rows)
    return out.reshape(rows, width)


def send_kernel(where, occ, virt, target, parts_ref, out_ref, total):
    turns = total.shape[0]
    for turn in range(turns):
        at = turn * VCAP
        added = parts_ref[0, :, at:at + VCAP].astype(F32)
        for x in range(1, 4):
            added = added + parts_ref[x, :, at:at + VCAP].astype(F32)
        total[turn] = added.astype(BF)
    mine = where[0]
    first = jnp.int32(0)
    for h in range(IRREPS):
        wide = columns_of(occ, virt, target, h)
        for e in range(2):
            begin = lax.shift_right_logical(first + 12 * e * wide, 7)
            p = begin + jnp.bitwise_and(mine - begin + 16 * ROWS, 15)
            out_ref[2 * h + e] = total[jnp.minimum(lax.shift_right_logical(p, 4), turns - 1)]
        first = first + occ[h] * wide


def send_out(parts, where, occ_count, virt_count, target):
    return pl.pallas_call(
        send_kernel,
        in_specs=[scalars()] * 4 + [pl.BlockSpec(memory_space=pltpu.VMEM)],
        out_specs=pl.BlockSpec(memory_space=pltpu.VMEM),
        out_shape=jax.ShapeDtypeStruct((ROWS, BLOCK, VCAP), BF),
        scratch_shapes=[pltpu.VMEM((parts.shape[2] // VCAP, BLOCK, VCAP), BF)],
        compiler_params=pltpu.CompilerParams(vmem_limit_bytes=24 << 20),
        name="send_out",
    )(where, occ_count, virt_count, target, parts)


def place_kernel(where, occ, virt, target, got_ref, out_ref):
    row, col = where[0], where[1]
    irrep, half = row // 2, row % 2
    first = first_column(occ, virt, target, irrep)
    wide = columns_of(occ, virt, target, irrep)
    line = col * BLOCK + lax.broadcasted_iota(jnp.int32, (BLOCK, VCAP), 0)
    b = lax.broadcasted_iota(jnp.int32, (BLOCK, VCAP), 1)
    inside = (line // VCAP < occ[0]) & (line % VCAP < virt[target[0]]) & (b < wide)
    for l in range(12):
        s = half * 12 + l
        at = first + s * wide
        p = lax.shift_right_logical(at, 7)
        shift = jnp.bitwise_and(at, 127)
        here = got_ref[jnp.bitwise_and(p, 15)].astype(F32)
        after = got_ref[jnp.bitwise_and(p + 1, 15)].astype(F32)
        block = jnp.where(b >= shift, here, after)
        block = pltpu.roll(block, jnp.bitwise_and(VCAP - shift, 127), 1)
        keep = inside & (s < occ[irrep])
        out_ref[:, l * VCAP:(l + 1) * VCAP] = jnp.where(keep, block, 0.0).astype(BF)


def place(got, where, occ_count, virt_count, target):
    return pl.pallas_call(
        place_kernel,
        in_specs=[scalars()] * 4 + [pl.BlockSpec(memory_space=pltpu.VMEM)],
        out_specs=pl.BlockSpec(memory_space=pltpu.VMEM),
        out_shape=jax.ShapeDtypeStruct((BLOCK, 12 * VCAP), BF),
        compiler_params=pltpu.CompilerParams(vmem_limit_bytes=32 << 20),
        name="place",
    )(where, occ_count, virt_count, target, got)


def bring(turns, dealt, *masks):
    landed = lax.all_to_all(dealt[SIZES.index(turns)], ("y", "core"), 0, 0, tiled=True)
    return repack(landed.reshape(ROWS * 6, turns, 8, VCAP), *masks)


def contract(turns, w_rows, t_rows, *masks):
    partial = product(turns, w_rows, t_rows)
    by_z = lax.psum_scatter(partial, "z", scatter_dimension=0, tiled=True)
    by_x = lax.all_to_all(by_z, "x", 0, 0, tiled=True).reshape(4, BLOCK, turns * VCAP)
    return lax.all_to_all(send_out(by_x, *masks), ("y", "core"), 0, 0, tiled=True)


def per_device(w_cycle, amplitudes, occ_count, virt_count, target):
    row = lax.axis_index("y") * 2 + lax.axis_index("core")
    col = lax.axis_index("x") * 8 + lax.axis_index("z")
    masks = (jnp.stack([row, col]).astype(jnp.int32), occ_count, virt_count, target)
    *dealt, which = deal(amplitudes, occ_count, virt_count, target)
    w_rows = lax.all_gather(w_cycle, ("y", "core"), axis=0, tiled=True)
    t_rows = lax.switch(
        which[0], [functools.partial(bring, turns) for turns in SIZES], dealt, *masks
    )
    got = lax.switch(
        which[0], [functools.partial(contract, turns) for turns in SIZES], w_rows, t_rows, *masks
    )
    return place(got, *masks)


def solution(mesh):
    chips = Mesh(mesh.devices.reshape(8, 2, 4, 8), ("y", "core", "x", "z"))
    row, col = ("y", "core"), ("x", "z")
    placed = (P(row, col), P(col, None, row, None), P(), P(), P())
    return jax.shard_map(
        per_device, mesh=chips, in_specs=placed, out_specs=P(col, row), check_vma=False
    )
```

```python
import functools

import jax
import jax.numpy as jnp
from jax import lax
from jax.experimental import pallas as pl
from jax.experimental.pallas import tpu as pltpu
from jax.sharding import Mesh, PartitionSpec as P

IRREPS = 8
OCAP = 24
VCAP = 128
KO = 192
ROWS = 16
SIZES = (5, 6, 8)
STEP = 12
BLOCK = 48
BF = jnp.bfloat16
F32 = jnp.float32


def scalars():
    return pl.BlockSpec(memory_space=pltpu.SMEM)


def columns_of(occ, virt, target, irrep):
    return virt[jnp.bitwise_xor(irrep, target[0])]


def first_column(occ, virt, target, irrep):
    total = jnp.int32(0)
    for h in range(IRREPS):
        total = total + jnp.where(h < irrep, occ[h] * columns_of(occ, virt, target, h), 0)
    return total


def size_class(pairs):
    return sum((pairs > (ROWS * turns - 1) * VCAP).astype(jnp.int32) for turns in SIZES[:-1])


def deal_kernel(occ, virt, target, t_ref, *rest):
    results, (class_ref, held, packed, sem, out_sem) = rest[:len(SIZES)], rest[len(SIZES):]
    copies = [
        pltpu.make_async_copy(
            t_ref.at[:, h * OCAP:(h + 1) * OCAP], held.at[:, h * OCAP:(h + 1) * OCAP], sem.at[h]
        )
        for h in range(IRREPS)
    ]
    for copy in copies:
        copy.start()
    lane = lax.broadcasted_iota(jnp.int32, (48, VCAP), 1)

    def put(p, value):
        packed[jnp.bitwise_and(p, 15), :, lax.shift_right_logical(p, 4)] = (
            value.astype(BF).reshape(6, 8, VCAP)
        )

    current = jnp.zeros((48, VCAP), F32)
    first = jnp.int32(0)
    for h in range(IRREPS):
        copies[h].wait()
        many = occ[h]
        wide = columns_of(occ, virt, target, h)

        def some(g, current, h=h, first=first, many=many, wide=wide):
            for u in range(STEP):
                s = g * STEP + u
                at = first + jnp.minimum(s, many) * wide
                shift = jnp.bitwise_and(at, 127)
                value = held[:, h * OCAP + s].astype(F32).reshape(48, VCAP)
                value = pltpu.roll(value, shift, 1)
                current = jnp.where(lane >= shift, value, current)
                put(lax.shift_right_logical(at, 7), current)
                current = jnp.where((s < many) & (shift + wide >= VCAP), value, current)
            return current

        current = lax.fori_loop(0, (many + STEP - 1) // STEP, some, current)
        first = first + many * wide
    put(lax.shift_right_logical(first, 7), current)
    which = size_class(first)
    class_ref[0] = which
    for n, turns in enumerate(SIZES):
        @pl.when(which == n)
        def _(n=n, turns=turns):
            copy = pltpu.make_async_copy(packed.at[:, :, :turns], results[n], out_sem)
            copy.start()
            copy.wait()


def deal(amplitudes, occ_count, virt_count, target):
    return pl.pallas_call(
        deal_kernel,
        in_specs=[scalars()] * 3 + [pl.BlockSpec(memory_space=pl.ANY)],
        out_specs=[pl.BlockSpec(memory_space=pl.ANY)] * len(SIZES) + [scalars()],
        out_shape=[jax.ShapeDtypeStruct((ROWS, 6, turns, 8, VCAP), BF) for turns in SIZES]
        + [jax.ShapeDtypeStruct((1,), jnp.int32)],
        scratch_shapes=[
            pltpu.VMEM((6, KO, 8, VCAP), BF),
            pltpu.VMEM((ROWS, 6, SIZES[-1], 8, VCAP), BF),
            pltpu.SemaphoreType.DMA((IRREPS,)),
            pltpu.SemaphoreType.DMA,
        ],
        compiler_params=pltpu.CompilerParams(vmem_limit_bytes=56 << 20),
        name="deal",
    )(occ_count, virt_count, target, amplitudes)


def repack_kernel(where, occ, virt, target, t_ref, out_ref):
    first_k = where[1] * 6
    irrep = first_k // OCAP
    k_base = first_k - irrep * OCAP
    n_occ = occ[irrep]
    n_virt = columns_of(occ, virt, target, irrep)
    c = lax.broadcasted_iota(jnp.int32, (VCAP, VCAP), 0)
    for turn in range(t_ref.shape[1]):
        held = t_ref[:, turn].astype(F32).reshape(ROWS, 6, 8, VCAP)
        for k in range(6):
            limit = jnp.where(k_base + k < n_occ, n_virt, 0)
            value = jnp.where(c < limit, held[:, k].reshape(VCAP, VCAP), 0.0)
            out_ref[k * VCAP:(k + 1) * VCAP, turn * VCAP:(turn + 1) * VCAP] = value.astype(BF)


def repack(landed, where, occ_count, virt_count, target):
    return pl.pallas_call(
        repack_kernel,
        in_specs=[scalars()] * 4 + [pl.BlockSpec(memory_space=pltpu.VMEM)],
        out_specs=pl.BlockSpec(memory_space=pltpu.VMEM),
        out_shape=jax.ShapeDtypeStruct((6 * VCAP, SIZES[-1] * VCAP), BF),
        compiler_params=pltpu.CompilerParams(vmem_limit_bytes=24 << 20),
        name="repack",
    )(where, occ_count, virt_count, target, landed)


def product_kernel(w_ref, t_ref, out_ref, w_held, held, w_sem, sem):
    tall, width = 4 * BLOCK, held.shape[3]
    arrivals = [
        pltpu.make_async_copy(
            w_ref.at[n * tall:(n + 1) * tall], w_held.at[n * tall:(n + 1) * tall], w_sem.at[n]
        )
        for n in range(8)
    ]
    for copy in arrivals:
        copy.start()
    copies = []
    for n in range(8):
        arrivals[n].wait()
        value = jnp.dot(
            w_held[n * tall:(n + 1) * tall, :], t_ref[:, :width], preferred_element_type=F32
        )
        for z in range(4):
            held[n, z] = value[z * BLOCK:(z + 1) * BLOCK].astype(BF)
        begin = 4 * (n % 2)
        copy = pltpu.make_async_copy(held.at[n], out_ref.at[begin:begin + 4, n // 2], sem.at[n])
        copy.start()
        copies.append(copy)
    for copy in copies:
        copy.wait()


def product(turns, w_rows, t_rows):
    rows, depth = w_rows.shape
    width = turns * VCAP
    out = pl.pallas_call(
        product_kernel,
        in_specs=[pl.BlockSpec(memory_space=pl.ANY), pl.BlockSpec(memory_space=pltpu.VMEM)],
        out_specs=pl.BlockSpec(memory_space=pl.ANY),
        out_shape=jax.ShapeDtypeStruct((8, 4, BLOCK, width), BF),
        scratch_shapes=[
            pltpu.VMEM((rows, depth), BF),
            pltpu.VMEM((8, 4, BLOCK, width), BF),
            pltpu.SemaphoreType.DMA((8,)),
            pltpu.SemaphoreType.DMA((8,)),
        ],
        compiler_params=pltpu.CompilerParams(vmem_limit_bytes=56 << 20),
        name="product",
    )(w_rows, t_rows)
    return out.reshape(8, rows // 8, width)


def send_kernel(where, occ, virt, target, parts_ref, out_ref, total):
    turns = total.shape[0]
    for turn in range(turns):
        at = turn * VCAP
        added = parts_ref[0, :, at:at + VCAP].astype(F32)
        for x in range(1, 4):
            added = added + parts_ref[x, :, at:at + VCAP].astype(F32)
        total[turn] = added.astype(BF)
    mine = where[0]
    first = jnp.int32(0)
    for h in range(IRREPS):
        wide = columns_of(occ, virt, target, h)
        for e in range(2):
            begin = lax.shift_right_logical(first + 12 * e * wide, 7)
            p = begin + jnp.bitwise_and(mine - begin + 16 * ROWS, 15)
            out_ref[2 * h + e] = total[jnp.minimum(lax.shift_right_logical(p, 4), turns - 1)]
        first = first + occ[h] * wide


def send_out(parts, where, occ_count, virt_count, target):
    return pl.pallas_call(
        send_kernel,
        in_specs=[scalars()] * 4 + [pl.BlockSpec(memory_space=pltpu.VMEM)],
        out_specs=pl.BlockSpec(memory_space=pltpu.VMEM),
        out_shape=jax.ShapeDtypeStruct((ROWS, BLOCK, VCAP), BF),
        scratch_shapes=[pltpu.VMEM((parts.shape[2] // VCAP, BLOCK, VCAP), BF)],
        compiler_params=pltpu.CompilerParams(vmem_limit_bytes=24 << 20),
        name="send_out",
    )(where, occ_count, virt_count, target, parts)


def place_kernel(where, occ, virt, target, got_ref, out_ref):
    row, col = where[0], where[1]
    irrep, half = row // 2, row % 2
    first = first_column(occ, virt, target, irrep)
    wide = columns_of(occ, virt, target, irrep)
    line = col * BLOCK + lax.broadcasted_iota(jnp.int32, (BLOCK, VCAP), 0)
    b = lax.broadcasted_iota(jnp.int32, (BLOCK, VCAP), 1)
    inside = (line // VCAP < occ[0]) & (line % VCAP < virt[target[0]]) & (b < wide)
    for l in range(12):
        s = half * 12 + l
        at = first + s * wide
        p = lax.shift_right_logical(at, 7)
        shift = jnp.bitwise_and(at, 127)
        here = got_ref[jnp.bitwise_and(p, 15)].astype(F32)
        after = got_ref[jnp.bitwise_and(p + 1, 15)].astype(F32)
        block = jnp.where(b >= shift, here, after)
        block = pltpu.roll(block, jnp.bitwise_and(VCAP - shift, 127), 1)
        keep = inside & (s < occ[irrep])
        out_ref[:, l * VCAP:(l + 1) * VCAP] = jnp.where(keep, block, 0.0).astype(BF)


def place(got, where, occ_count, virt_count, target):
    return pl.pallas_call(
        place_kernel,
        in_specs=[scalars()] * 4 + [pl.BlockSpec(memory_space=pltpu.VMEM)],
        out_specs=pl.BlockSpec(memory_space=pltpu.VMEM),
        out_shape=jax.ShapeDtypeStruct((BLOCK, 12 * VCAP), BF),
        compiler_params=pltpu.CompilerParams(vmem_limit_bytes=32 << 20),
        name="place",
    )(where, occ_count, virt_count, target, got)


def bring(turns, dealt, *masks):
    landed = lax.all_to_all(dealt[SIZES.index(turns)], ("y", "core"), 0, 0, tiled=True)
    return repack(landed.reshape(ROWS * 6, turns, 8, VCAP), *masks)


def contract(turns, w_rows, t_rows, *masks):
    partial = product(turns, w_rows, t_rows)
    by_z = lax.psum_scatter(partial, "z", scatter_dimension=0, tiled=True)
    by_z = by_z.reshape(4, BLOCK, turns * VCAP)
    by_x = lax.all_to_all(by_z, "x", 0, 0, tiled=True)
    return lax.all_to_all(send_out(by_x, *masks), ("y", "core"), 0, 0, tiled=True)


def per_device(w_cycle, amplitudes, occ_count, virt_count, target):
    row = lax.axis_index("y") * 2 + lax.axis_index("core")
    col = lax.axis_index("x") * 8 + lax.axis_index("z")
    masks = (jnp.stack([row, col]).astype(jnp.int32), occ_count, virt_count, target)
    *dealt, which = deal(amplitudes, occ_count, virt_count, target)
    w_rows = lax.all_gather(w_cycle, ("y", "core"), axis=0, tiled=True)
    t_rows = lax.switch(
        which[0], [functools.partial(bring, turns) for turns in SIZES], dealt, *masks
    )
    got = lax.switch(
        which[0], [functools.partial(contract, turns) for turns in SIZES], w_rows, t_rows, *masks
    )
    return place(got, *masks)


def solution(mesh):
    chips = Mesh(mesh.devices.reshape(8, 2, 4, 8), ("y", "core", "x", "z"))
    row, col = ("y", "core"), ("x", "z")
    placed = (P(row, col), P(col, None, row, None), P(), P(), P())
    return jax.shard_map(
        per_device, mesh=chips, in_specs=placed, out_specs=P(col, row), check_vma=False
    )
```

```python
import functools

import jax
import jax.numpy as jnp
from jax import lax
from jax.experimental import pallas as pl
from jax.experimental.pallas import tpu as pltpu
from jax.sharding import Mesh, PartitionSpec as P

IRREPS = 8
OCAP = 24
VCAP = 128
KO = 192
ROWS = 16
SIZES = (5, 6, 8)
STEP = 12
BLOCK = 48
BF = jnp.bfloat16
F32 = jnp.float32


def scalars():
    return pl.BlockSpec(memory_space=pltpu.SMEM)


def columns_of(occ, virt, target, irrep):
    return virt[jnp.bitwise_xor(irrep, target[0])]


def first_column(occ, virt, target, irrep):
    total = jnp.int32(0)
    for h in range(IRREPS):
        total = total + jnp.where(h < irrep, occ[h] * columns_of(occ, virt, target, h), 0)
    return total


def size_class(pairs):
    return sum((pairs > ROWS * turns * VCAP).astype(jnp.int32) for turns in SIZES[:-1])


def deal_kernel(occ, virt, target, t_ref, *rest):
    results, (class_ref, held, packed, sem, out_sem) = rest[:len(SIZES)], rest[len(SIZES):]
    copies = [
        pltpu.make_async_copy(
            t_ref.at[:, h * OCAP:(h + 1) * OCAP], held.at[:, h * OCAP:(h + 1) * OCAP], sem.at[h]
        )
        for h in range(IRREPS)
    ]
    for copy in copies:
        copy.start()
    lane = lax.broadcasted_iota(jnp.int32, (48, VCAP), 1)

    def put(p, value):
        packed[jnp.bitwise_and(p, 15), :, lax.shift_right_logical(p, 4)] = (
            value.astype(BF).reshape(6, 8, VCAP)
        )

    current = jnp.zeros((48, VCAP), F32)
    first = jnp.int32(0)
    for h in range(IRREPS):
        copies[h].wait()
        many = occ[h]
        wide = columns_of(occ, virt, target, h)

        def some(g, current, h=h, first=first, many=many, wide=wide):
            for u in range(STEP):
                s = g * STEP + u
                at = first + jnp.minimum(s, many) * wide
                shift = jnp.bitwise_and(at, 127)
                value = held[:, h * OCAP + s].astype(F32).reshape(48, VCAP)
                value = pltpu.roll(value, shift, 1)
                current = jnp.where(lane >= shift, value, current)
                put(lax.shift_right_logical(at, 7), current)
                current = jnp.where((s < many) & (shift + wide >= VCAP), value, current)
            return current

        current = lax.fori_loop(0, (many + STEP - 1) // STEP, some, current)
        first = first + many * wide
    put(lax.shift_right_logical(first, 7), current)
    which = size_class(first)
    class_ref[0] = which
    for n, turns in enumerate(SIZES):
        @pl.when(which == n)
        def _(n=n, turns=turns):
            copy = pltpu.make_async_copy(packed.at[:, :, :turns], results[n], out_sem)
            copy.start()
            copy.wait()


def deal(amplitudes, occ_count, virt_count, target):
    return pl.pallas_call(
        deal_kernel,
        in_specs=[scalars()] * 3 + [pl.BlockSpec(memory_space=pl.ANY)],
        out_specs=[pl.BlockSpec(memory_space=pl.ANY)] * len(SIZES) + [scalars()],
        out_shape=[jax.ShapeDtypeStruct((ROWS, 6, turns, 8, VCAP), BF) for turns in SIZES]
        + [jax.ShapeDtypeStruct((1,), jnp.int32)],
        scratch_shapes=[
            pltpu.VMEM((6, KO, 8, VCAP), BF),
            pltpu.VMEM((ROWS, 6, SIZES[-1], 8, VCAP), BF),
            pltpu.SemaphoreType.DMA((IRREPS,)),
            pltpu.SemaphoreType.DMA,
        ],
        compiler_params=pltpu.CompilerParams(vmem_limit_bytes=56 << 20),
        name="deal",
    )(occ_count, virt_count, target, amplitudes)


def repack_kernel(where, occ, virt, target, t_ref, out_ref):
    first_k = where[1] * 6
    irrep = first_k // OCAP
    k_base = first_k - irrep * OCAP
    n_occ = occ[irrep]
    n_virt = columns_of(occ, virt, target, irrep)
    c = lax.broadcasted_iota(jnp.int32, (VCAP, VCAP), 0)
    for turn in range(t_ref.shape[1]):
        held = t_ref[:, turn].astype(F32).reshape(ROWS, 6, 8, VCAP)
        for k in range(6):
            limit = jnp.where(k_base + k < n_occ, n_virt, 0)
            value = jnp.where(c < limit, held[:, k].reshape(VCAP, VCAP), 0.0)
            out_ref[k * VCAP:(k + 1) * VCAP, turn * VCAP:(turn + 1) * VCAP] = value.astype(BF)


def repack(landed, where, occ_count, virt_count, target):
    return pl.pallas_call(
        repack_kernel,
        in_specs=[scalars()] * 4 + [pl.BlockSpec(memory_space=pltpu.VMEM)],
        out_specs=pl.BlockSpec(memory_space=pltpu.VMEM),
        out_shape=jax.ShapeDtypeStruct((6 * VCAP, SIZES[-1] * VCAP), BF),
        compiler_params=pltpu.CompilerParams(vmem_limit_bytes=24 << 20),
        name="repack",
    )(where, occ_count, virt_count, target, landed)


def product_kernel(w_ref, t_ref, out_ref, held, sem):
    tall, width = 4 * BLOCK, held.shape[3]
    copies = []
    for n in range(8):
        value = jnp.dot(
            w_ref[n * tall:(n + 1) * tall, :], t_ref[:, :width], preferred_element_type=F32
        )
        for z in range(4):
            held[n, z] = value[z * BLOCK:(z + 1) * BLOCK].astype(BF)
        begin = 4 * (n % 2)
        copy = pltpu.make_async_copy(held.at[n], out_ref.at[begin:begin + 4, n // 2], sem.at[n])
        copy.start()
        copies.append(copy)
    for copy in copies:
        copy.wait()


def product(turns, w_rows, t_rows):
    rows = w_rows.shape[0]
    width = turns * VCAP
    out = pl.pallas_call(
        product_kernel,
        in_specs=[pl.BlockSpec(memory_space=pltpu.VMEM)] * 2,
        out_specs=pl.BlockSpec(memory_space=pl.ANY),
        out_shape=jax.ShapeDtypeStruct((8, 4, BLOCK, width), BF),
        scratch_shapes=[pltpu.VMEM((8, 4, BLOCK, width), BF), pltpu.SemaphoreType.DMA((8,))],
        compiler_params=pltpu.CompilerParams(vmem_limit_bytes=24 << 20),
        name="product",
    )(w_rows, t_rows)
    return out.reshape(8, rows // 8, width)


def send_kernel(where, occ, virt, target, parts_ref, out_ref, total):
    turns = total.shape[0]
    for turn in range(turns):
        at = turn * VCAP
        added = parts_ref[0, :, at:at + VCAP].astype(F32)
        for x in range(1, 4):
            added = added + parts_ref[x, :, at:at + VCAP].astype(F32)
        total[turn] = added.astype(BF)
    mine = where[0]
    first = jnp.int32(0)
    for h in range(IRREPS):
        wide = columns_of(occ, virt, target, h)
        for e in range(2):
            begin = lax.shift_right_logical(first + 12 * e * wide, 7)
            p = begin + jnp.bitwise_and(mine - begin + 16 * ROWS, 15)
            out_ref[2 * h + e] = total[jnp.minimum(lax.shift_right_logical(p, 4), turns - 1)]
        first = first + occ[h] * wide


def send_out(parts, where, occ_count, virt_count, target):
    return pl.pallas_call(
        send_kernel,
        in_specs=[scalars()] * 4 + [pl.BlockSpec(memory_space=pltpu.VMEM)],
        out_specs=pl.BlockSpec(memory_space=pltpu.VMEM),
        out_shape=jax.ShapeDtypeStruct((ROWS, BLOCK, VCAP), BF),
        scratch_shapes=[pltpu.VMEM((parts.shape[2] // VCAP, BLOCK, VCAP), BF)],
        compiler_params=pltpu.CompilerParams(vmem_limit_bytes=24 << 20),
        name="send_out",
    )(where, occ_count, virt_count, target, parts)


def place_kernel(where, occ, virt, target, got_ref, out_ref):
    row, col = where[0], where[1]
    irrep, half = row // 2, row % 2
    first = first_column(occ, virt, target, irrep)
    wide = columns_of(occ, virt, target, irrep)
    line = col * BLOCK + lax.broadcasted_iota(jnp.int32, (BLOCK, VCAP), 0)
    b = lax.broadcasted_iota(jnp.int32, (BLOCK, VCAP), 1)
    inside = (line // VCAP < occ[0]) & (line % VCAP < virt[target[0]]) & (b < wide)
    for l in range(12):
        s = half * 12 + l
        at = first + s * wide
        p = lax.shift_right_logical(at, 7)
        shift = jnp.bitwise_and(at, 127)
        here = got_ref[jnp.bitwise_and(p, 15)].astype(F32)
        after = got_ref[jnp.bitwise_and(p + 1, 15)].astype(F32)
        block = jnp.where(b >= shift, here, after)
        block = pltpu.roll(block, jnp.bitwise_and(VCAP - shift, 127), 1)
        keep = inside & (s < occ[irrep])
        out_ref[:, l * VCAP:(l + 1) * VCAP] = jnp.where(keep, block, 0.0).astype(BF)


def place(got, where, occ_count, virt_count, target):
    return pl.pallas_call(
        place_kernel,
        in_specs=[scalars()] * 4 + [pl.BlockSpec(memory_space=pltpu.VMEM)],
        out_specs=pl.BlockSpec(memory_space=pltpu.VMEM),
        out_shape=jax.ShapeDtypeStruct((BLOCK, 12 * VCAP), BF),
        compiler_params=pltpu.CompilerParams(vmem_limit_bytes=32 << 20),
        name="place",
    )(where, occ_count, virt_count, target, got)


def bring(turns, dealt, *masks):
    landed = lax.all_to_all(dealt[SIZES.index(turns)], ("y", "core"), 0, 0, tiled=True)
    return repack(landed.reshape(ROWS * 6, turns, 8, VCAP), *masks)


def contract(turns, w_rows, t_rows, *masks):
    partial = product(turns, w_rows, t_rows)
    by_z = lax.psum_scatter(partial, "z", scatter_dimension=0, tiled=True)
    by_x = lax.all_to_all(by_z.reshape(4, BLOCK, turns * VCAP), "x", 0, 0, tiled=True)
    return lax.all_to_all(send_out(by_x, *masks), ("y", "core"), 0, 0, tiled=True)


def per_device(w_cycle, amplitudes, occ_count, virt_count, target):
    row = lax.axis_index("y") * 2 + lax.axis_index("core")
    col = lax.axis_index("x") * 8 + lax.axis_index("z")
    masks = (jnp.stack([row, col]).astype(jnp.int32), occ_count, virt_count, target)
    *dealt, which = deal(amplitudes, occ_count, virt_count, target)
    w_rows = lax.all_gather(w_cycle, ("y", "core"), axis=0, tiled=True)
    t_rows = lax.switch(
        which[0], [functools.partial(bring, turns) for turns in SIZES], dealt, *masks
    )
    got = lax.switch(
        which[0], [functools.partial(contract, turns) for turns in SIZES], w_rows, t_rows, *masks
    )
    return place(got, *masks)


def solution(mesh):
    chips = Mesh(mesh.devices.reshape(8, 2, 4, 8), ("y", "core", "x", "z"))
    row, col = ("y", "core"), ("x", "z")
    placed = (P(row, col), P(col, None, row, None), P(), P(), P())
    return jax.shard_map(
        per_device, mesh=chips, in_specs=placed, out_specs=P(col, row), check_vma=False
    )
```

```python
import functools

import jax
import jax.numpy as jnp
from jax import lax
from jax.experimental import pallas as pl
from jax.experimental.pallas import tpu as pltpu
from jax.sharding import Mesh, PartitionSpec as P

IRREPS = 8
OCAP = 24
VCAP = 128
KO = 192
ROWS = 16
SIZES = (5, 6, 8)
STEP = 12
BLOCK = 48
BF = jnp.bfloat16
F32 = jnp.float32


def scalars():
    return pl.BlockSpec(memory_space=pltpu.SMEM)


def columns_of(occ, virt, target, irrep):
    return virt[jnp.bitwise_xor(irrep, target[0])]


def first_column(occ, virt, target, irrep):
    total = jnp.int32(0)
    for h in range(IRREPS):
        total = total + jnp.where(h < irrep, occ[h] * columns_of(occ, virt, target, h), 0)
    return total


def size_class(pairs):
    return sum((pairs >= ROWS * turns * VCAP).astype(jnp.int32) for turns in SIZES[:-1])


def pack(occ, virt, target, held, copies, out_ref):
    lane = lax.broadcasted_iota(jnp.int32, (48, VCAP), 1)

    def put(p, value):
        out_ref[jnp.bitwise_and(p, 15), :, lax.shift_right_logical(p, 4)] = (
            value.astype(BF).reshape(6, 8, VCAP)
        )

    current = jnp.zeros((48, VCAP), F32)
    first = jnp.int32(0)
    for h in range(IRREPS):
        copies[h].wait()
        many = occ[h]
        wide = columns_of(occ, virt, target, h)

        def some(g, current, h=h, first=first, many=many, wide=wide):
            for u in range(STEP):
                s = g * STEP + u
                at = first + jnp.minimum(s, many) * wide
                shift = jnp.bitwise_and(at, 127)
                value = held[:, h * OCAP + s].astype(F32).reshape(48, VCAP)
                value = pltpu.roll(value, shift, 1)
                current = jnp.where(lane >= shift, value, current)
                put(lax.shift_right_logical(at, 7), current)
                current = jnp.where((s < many) & (shift + wide >= VCAP), value, current)
            return current

        current = lax.fori_loop(0, (many + STEP - 1) // STEP, some, current)
        first = first + many * wide
    put(lax.shift_right_logical(first, 7), current)


def deal_kernel(occ, virt, target, t_ref, *rest):
    results, (class_ref, held, sem) = rest[:len(SIZES)], rest[len(SIZES):]
    copies = [
        pltpu.make_async_copy(
            t_ref.at[:, h * OCAP:(h + 1) * OCAP], held.at[:, h * OCAP:(h + 1) * OCAP], sem.at[h]
        )
        for h in range(IRREPS)
    ]
    for copy in copies:
        copy.start()
    which = size_class(first_column(occ, virt, target, IRREPS))
    class_ref[0] = which
    for n in range(len(SIZES)):
        @pl.when(which == n)
        def _(n=n):
            pack(occ, virt, target, held, copies, results[n])


def deal(amplitudes, occ_count, virt_count, target):
    return pl.pallas_call(
        deal_kernel,
        in_specs=[scalars()] * 3 + [pl.BlockSpec(memory_space=pl.ANY)],
        out_specs=[pl.BlockSpec(memory_space=pltpu.VMEM)] * len(SIZES) + [scalars()],
        out_shape=[jax.ShapeDtypeStruct((ROWS, 6, turns, 8, VCAP), BF) for turns in SIZES]
        + [jax.ShapeDtypeStruct((1,), jnp.int32)],
        scratch_shapes=[
            pltpu.VMEM((6, KO, 8, VCAP), BF),
            pltpu.SemaphoreType.DMA((IRREPS,)),
        ],
        compiler_params=pltpu.CompilerParams(vmem_limit_bytes=56 << 20),
        name="deal",
    )(occ_count, virt_count, target, amplitudes)


def repack_kernel(where, occ, virt, target, t_ref, out_ref):
    first_k = where[1] * 6
    irrep = first_k // OCAP
    k_base = first_k - irrep * OCAP
    n_occ = occ[irrep]
    n_virt = columns_of(occ, virt, target, irrep)
    c = lax.broadcasted_iota(jnp.int32, (VCAP, VCAP), 0)
    for turn in range(t_ref.shape[1]):
        held = t_ref[:, turn].astype(F32).reshape(ROWS, 6, 8, VCAP)
        for k in range(6):
            limit = jnp.where(k_base + k < n_occ, n_virt, 0)
            value = jnp.where(c < limit, held[:, k].reshape(VCAP, VCAP), 0.0)
            out_ref[k * VCAP:(k + 1) * VCAP, turn * VCAP:(turn + 1) * VCAP] = value.astype(BF)


def repack(landed, where, occ_count, virt_count, target):
    return pl.pallas_call(
        repack_kernel,
        in_specs=[scalars()] * 4 + [pl.BlockSpec(memory_space=pltpu.VMEM)],
        out_specs=pl.BlockSpec(memory_space=pltpu.VMEM),
        out_shape=jax.ShapeDtypeStruct((6 * VCAP, SIZES[-1] * VCAP), BF),
        compiler_params=pltpu.CompilerParams(vmem_limit_bytes=24 << 20),
        name="repack",
    )(where, occ_count, virt_count, target, landed)


def product_kernel(w_ref, t_ref, out_ref, held, sem):
    tall, width = 4 * BLOCK, held.shape[3]
    copies = []
    for n in range(8):
        value = jnp.dot(
            w_ref[n * tall:(n + 1) * tall, :], t_ref[:, :width], preferred_element_type=F32
        )
        for z in range(4):
            held[n, z] = value[z * BLOCK:(z + 1) * BLOCK].astype(BF)
        begin = 4 * (n % 2)
        copy = pltpu.make_async_copy(held.at[n], out_ref.at[begin:begin + 4, n // 2], sem.at[n])
        copy.start()
        copies.append(copy)
    for copy in copies:
        copy.wait()


def product(turns, w_rows, t_rows):
    rows = w_rows.shape[0]
    width = turns * VCAP
    out = pl.pallas_call(
        product_kernel,
        in_specs=[pl.BlockSpec(memory_space=pltpu.VMEM)] * 2,
        out_specs=pl.BlockSpec(memory_space=pl.ANY),
        out_shape=jax.ShapeDtypeStruct((8, 4, BLOCK, width), BF),
        scratch_shapes=[pltpu.VMEM((8, 4, BLOCK, width), BF), pltpu.SemaphoreType.DMA((8,))],
        compiler_params=pltpu.CompilerParams(vmem_limit_bytes=24 << 20),
        name="product",
    )(w_rows, t_rows)
    return out.reshape(8, rows // 8, width)


def send_kernel(where, occ, virt, target, parts_ref, out_ref, total):
    turns = total.shape[0]
    for turn in range(turns):
        at = turn * VCAP
        added = parts_ref[0, :, at:at + VCAP].astype(F32)
        for x in range(1, 4):
            added = added + parts_ref[x, :, at:at + VCAP].astype(F32)
        total[turn] = added.astype(BF)
    mine = where[0]
    first = jnp.int32(0)
    for h in range(IRREPS):
        wide = columns_of(occ, virt, target, h)
        for e in range(2):
            begin = lax.shift_right_logical(first + 12 * e * wide, 7)
            p = begin + jnp.bitwise_and(mine - begin + 16 * ROWS, 15)
            out_ref[2 * h + e] = total[jnp.minimum(lax.shift_right_logical(p, 4), turns - 1)]
        first = first + occ[h] * wide


def send_out(parts, where, occ_count, virt_count, target):
    return pl.pallas_call(
        send_kernel,
        in_specs=[scalars()] * 4 + [pl.BlockSpec(memory_space=pltpu.VMEM)],
        out_specs=pl.BlockSpec(memory_space=pltpu.VMEM),
        out_shape=jax.ShapeDtypeStruct((ROWS, BLOCK, VCAP), BF),
        scratch_shapes=[pltpu.VMEM((parts.shape[2] // VCAP, BLOCK, VCAP), BF)],
        compiler_params=pltpu.CompilerParams(vmem_limit_bytes=24 << 20),
        name="send_out",
    )(where, occ_count, virt_count, target, parts)


def place_kernel(where, occ, virt, target, got_ref, out_ref):
    row, col = where[0], where[1]
    irrep, half = row // 2, row % 2
    first = first_column(occ, virt, target, irrep)
    wide = columns_of(occ, virt, target, irrep)
    line = col * BLOCK + lax.broadcasted_iota(jnp.int32, (BLOCK, VCAP), 0)
    b = lax.broadcasted_iota(jnp.int32, (BLOCK, VCAP), 1)
    inside = (line // VCAP < occ[0]) & (line % VCAP < virt[target[0]]) & (b < wide)
    for l in range(12):
        s = half * 12 + l
        at = first + s * wide
        p = lax.shift_right_logical(at, 7)
        shift = jnp.bitwise_and(at, 127)
        here = got_ref[jnp.bitwise_and(p, 15)].astype(F32)
        after = got_ref[jnp.bitwise_and(p + 1, 15)].astype(F32)
        block = jnp.where(b >= shift, here, after)
        block = pltpu.roll(block, jnp.bitwise_and(VCAP - shift, 127), 1)
        keep = inside & (s < occ[irrep])
        out_ref[:, l * VCAP:(l + 1) * VCAP] = jnp.where(keep, block, 0.0).astype(BF)


def place(got, where, occ_count, virt_count, target):
    return pl.pallas_call(
        place_kernel,
        in_specs=[scalars()] * 4 + [pl.BlockSpec(memory_space=pltpu.VMEM)],
        out_specs=pl.BlockSpec(memory_space=pltpu.VMEM),
        out_shape=jax.ShapeDtypeStruct((BLOCK, 12 * VCAP), BF),
        compiler_params=pltpu.CompilerParams(vmem_limit_bytes=32 << 20),
        name="place",
    )(where, occ_count, virt_count, target, got)


def bring(turns, dealt, *masks):
    landed = lax.all_to_all(dealt[SIZES.index(turns)], ("y", "core"), 0, 0, tiled=True)
    return repack(landed.reshape(ROWS * 6, turns, 8, VCAP), *masks)


def contract(turns, w_rows, t_rows, *masks):
    partial = product(turns, w_rows, t_rows)
    by_z = lax.psum_scatter(partial, "z", scatter_dimension=0, tiled=True)
    by_x = lax.all_to_all(by_z.reshape(4, BLOCK, turns * VCAP), "x", 0, 0, tiled=True)
    return lax.all_to_all(send_out(by_x, *masks), ("y", "core"), 0, 0, tiled=True)


def per_device(w_cycle, amplitudes, occ_count, virt_count, target):
    row = lax.axis_index("y") * 2 + lax.axis_index("core")
    col = lax.axis_index("x") * 8 + lax.axis_index("z")
    masks = (jnp.stack([row, col]).astype(jnp.int32), occ_count, virt_count, target)
    *dealt, which = deal(amplitudes, occ_count, virt_count, target)
    w_rows = lax.all_gather(w_cycle, ("y", "core"), axis=0, tiled=True)
    t_rows = lax.switch(
        which[0], [functools.partial(bring, turns) for turns in SIZES], dealt, *masks
    )
    got = lax.switch(
        which[0], [functools.partial(contract, turns) for turns in SIZES], w_rows, t_rows, *masks
    )
    return place(got, *masks)


def solution(mesh):
    chips = Mesh(mesh.devices.reshape(8, 2, 4, 8), ("y", "core", "x", "z"))
    row, col = ("y", "core"), ("x", "z")
    placed = (P(row, col), P(col, None, row, None), P(), P(), P())
    return jax.shard_map(
        per_device, mesh=chips, in_specs=placed, out_specs=P(col, row), check_vma=False
    )
```

```python
import functools

import jax
import jax.numpy as jnp
from jax import lax
from jax.experimental import pallas as pl
from jax.experimental.pallas import tpu as pltpu
from jax.sharding import Mesh, PartitionSpec as P

IRREPS = 8
OCAP = 24
VCAP = 128
KO = 192
ROWS = 16
SIZES = (5, 6, 8)
STEP = 12
BLOCK = 48
BF = jnp.bfloat16
F32 = jnp.float32


def scalars():
    return pl.BlockSpec(memory_space=pltpu.SMEM)


def columns_of(occ, virt, target, irrep):
    return virt[jnp.bitwise_xor(irrep, target[0])]


def first_column(occ, virt, target, irrep):
    total = jnp.int32(0)
    for h in range(IRREPS):
        total = total + jnp.where(h < irrep, occ[h] * columns_of(occ, virt, target, h), 0)
    return total


def size_class(pairs):
    return sum((pairs > ROWS * turns * VCAP).astype(jnp.int32) for turns in SIZES[:-1])


def deal_kernel(occ, virt, target, t_ref, *rest):
    results, (class_ref, held, packed, sem, out_sem) = rest[:len(SIZES)], rest[len(SIZES):]
    copies = [
        pltpu.make_async_copy(
            t_ref.at[:, h * OCAP:(h + 1) * OCAP], held.at[:, h * OCAP:(h + 1) * OCAP], sem.at[h]
        )
        for h in range(IRREPS)
    ]
    for copy in copies:
        copy.start()
    lane = lax.broadcasted_iota(jnp.int32, (48, VCAP), 1)

    def put(p, value):
        packed[jnp.bitwise_and(p, 15), :, lax.shift_right_logical(p, 4)] = (
            value.astype(BF).reshape(6, 8, VCAP)
        )

    current = jnp.zeros((48, VCAP), F32)
    first = jnp.int32(0)
    for h in range(IRREPS):
        copies[h].wait()
        many = occ[h]
        wide = columns_of(occ, virt, target, h)

        def some(g, current, h=h, first=first, many=many, wide=wide):
            for u in range(STEP):
                s = g * STEP + u
                at = first + jnp.minimum(s, many) * wide
                shift = jnp.bitwise_and(at, 127)
                value = held[:, h * OCAP + s].astype(F32).reshape(48, VCAP)
                value = pltpu.roll(value, shift, 1)
                current = jnp.where(lane >= shift, value, current)
                put(lax.shift_right_logical(at, 7), current)
                current = jnp.where((s < many) & (shift + wide >= VCAP), value, current)
            return current

        current = lax.fori_loop(0, (many + STEP - 1) // STEP, some, current)
        first = first + many * wide
    put(lax.shift_right_logical(first, 7), current)
    which = size_class(first)
    class_ref[0] = which
    for n, turns in enumerate(SIZES):
        @pl.when(which == n)
        def _(n=n, turns=turns):
            copy = pltpu.make_async_copy(packed.at[:, :, :turns], results[n], out_sem)
            copy.start()
            copy.wait()


def deal(amplitudes, occ_count, virt_count, target):
    return pl.pallas_call(
        deal_kernel,
        in_specs=[scalars()] * 3 + [pl.BlockSpec(memory_space=pl.ANY)],
        out_specs=[pl.BlockSpec(memory_space=pl.ANY)] * len(SIZES) + [scalars()],
        out_shape=[jax.ShapeDtypeStruct((ROWS, 6, turns, 8, VCAP), BF) for turns in SIZES]
        + [jax.ShapeDtypeStruct((1,), jnp.int32)],
        scratch_shapes=[
            pltpu.VMEM((6, KO, 8, VCAP), BF),
            pltpu.VMEM((ROWS, 6, SIZES[-1], 8, VCAP), BF),
            pltpu.SemaphoreType.DMA((IRREPS,)),
            pltpu.SemaphoreType.DMA,
        ],
        compiler_params=pltpu.CompilerParams(vmem_limit_bytes=56 << 20),
        name="deal",
    )(occ_count, virt_count, target, amplitudes)


def repack_kernel(where, occ, virt, target, t_ref, out_ref):
    first_k = where[1] * 6
    irrep = first_k // OCAP
    k_base = first_k - irrep * OCAP
    n_occ = occ[irrep]
    n_virt = columns_of(occ, virt, target, irrep)
    c = lax.broadcasted_iota(jnp.int32, (VCAP, VCAP), 0)
    for turn in range(t_ref.shape[1]):
        held = t_ref[:, turn].astype(F32).reshape(ROWS, 6, 8, VCAP)
        for k in range(6):
            limit = jnp.where(k_base + k < n_occ, n_virt, 0)
            value = jnp.where(c < limit, held[:, k].reshape(VCAP, VCAP), 0.0)
            out_ref[k * VCAP:(k + 1) * VCAP, turn * VCAP:(turn + 1) * VCAP] = value.astype(BF)


def repack(landed, where, occ_count, virt_count, target):
    return pl.pallas_call(
        repack_kernel,
        in_specs=[scalars()] * 4 + [pl.BlockSpec(memory_space=pltpu.VMEM)],
        out_specs=pl.BlockSpec(memory_space=pltpu.VMEM),
        out_shape=jax.ShapeDtypeStruct((6 * VCAP, SIZES[-1] * VCAP), BF),
        compiler_params=pltpu.CompilerParams(vmem_limit_bytes=24 << 20),
        name="repack",
    )(where, occ_count, virt_count, target, landed)


def product_kernel(w_ref, t_ref, out_ref, held, sem):
    tall, width = 4 * BLOCK, held.shape[3]
    copies = []
    for n in range(8):
        value = jnp.dot(
            w_ref[n * tall:(n + 1) * tall, :], t_ref[:, :width], preferred_element_type=F32
        )
        for z in range(4):
            held[n, z] = value[z * BLOCK:(z + 1) * BLOCK].astype(BF)
        begin = 4 * (n % 2)
        copy = pltpu.make_async_copy(held.at[n], out_ref.at[begin:begin + 4, n // 2], sem.at[n])
        copy.start()
        copies.append(copy)
    for copy in copies:
        copy.wait()


def product(turns, w_rows, t_rows):
    rows = w_rows.shape[0]
    width = turns * VCAP
    out = pl.pallas_call(
        product_kernel,
        in_specs=[pl.BlockSpec(memory_space=pltpu.VMEM)] * 2,
        out_specs=pl.BlockSpec(memory_space=pl.ANY),
        out_shape=jax.ShapeDtypeStruct((8, 4, BLOCK, width), BF),
        scratch_shapes=[pltpu.VMEM((8, 4, BLOCK, width), BF), pltpu.SemaphoreType.DMA((8,))],
        compiler_params=pltpu.CompilerParams(vmem_limit_bytes=24 << 20),
        name="product",
    )(w_rows, t_rows)
    return out.reshape(8, rows // 8, width)


def send_kernel(where, occ, virt, target, parts_ref, out_ref):
    turns = parts_ref.shape[2] // VCAP
    mine = where[0]
    first = jnp.int32(0)
    for h in range(IRREPS):
        wide = columns_of(occ, virt, target, h)
        for e in range(2):
            begin = lax.shift_right_logical(first + 12 * e * wide, 7)
            p = begin + jnp.bitwise_and(mine - begin + 16 * ROWS, 15)
            turn = jnp.minimum(lax.shift_right_logical(p, 4), turns - 1)
            at = pl.ds(pl.multiple_of(turn * VCAP, VCAP), VCAP)
            for x in range(4):
                out_ref[4 * (2 * h + e) + x] = parts_ref[x, :, at]
        first = first + occ[h] * wide


def send_out(parts, where, occ_count, virt_count, target):
    return pl.pallas_call(
        send_kernel,
        in_specs=[scalars()] * 4 + [pl.BlockSpec(memory_space=pltpu.VMEM)],
        out_specs=pl.BlockSpec(memory_space=pltpu.VMEM),
        out_shape=jax.ShapeDtypeStruct((4 * ROWS, BLOCK, VCAP), BF),
        compiler_params=pltpu.CompilerParams(vmem_limit_bytes=24 << 20),
        name="send_out",
    )(where, occ_count, virt_count, target, parts)


def place_kernel(where, occ, virt, target, got_ref, out_ref, total):
    for q in range(ROWS):
        added = got_ref[4 * q].astype(F32)
        for x in range(1, 4):
            added = added + got_ref[4 * q + x].astype(F32)
        total[q] = added
    row, col = where[0], where[1]
    irrep, half = row // 2, row % 2
    first = first_column(occ, virt, target, irrep)
    wide = columns_of(occ, virt, target, irrep)
    line = col * BLOCK + lax.broadcasted_iota(jnp.int32, (BLOCK, VCAP), 0)
    b = lax.broadcasted_iota(jnp.int32, (BLOCK, VCAP), 1)
    inside = (line // VCAP < occ[0]) & (line % VCAP < virt[target[0]]) & (b < wide)
    for l in range(12):
        s = half * 12 + l
        at = first + s * wide
        p = lax.shift_right_logical(at, 7)
        shift = jnp.bitwise_and(at, 127)
        here = total[jnp.bitwise_and(p, 15)]
        after = total[jnp.bitwise_and(p + 1, 15)]
        block = jnp.where(b >= shift, here, after)
        block = pltpu.roll(block, jnp.bitwise_and(VCAP - shift, 127), 1)
        keep = inside & (s < occ[irrep])
        out_ref[:, l * VCAP:(l + 1) * VCAP] = jnp.where(keep, block, 0.0).astype(BF)


def place(got, where, occ_count, virt_count, target):
    return pl.pallas_call(
        place_kernel,
        in_specs=[scalars()] * 4 + [pl.BlockSpec(memory_space=pltpu.VMEM)],
        out_specs=pl.BlockSpec(memory_space=pltpu.VMEM),
        out_shape=jax.ShapeDtypeStruct((BLOCK, 12 * VCAP), BF),
        scratch_shapes=[pltpu.VMEM((ROWS, BLOCK, VCAP), F32)],
        compiler_params=pltpu.CompilerParams(vmem_limit_bytes=32 << 20),
        name="place",
    )(where, occ_count, virt_count, target, got)


def bring(turns, dealt, *masks):
    landed = lax.all_to_all(dealt[SIZES.index(turns)], ("y", "core"), 0, 0, tiled=True)
    return repack(landed.reshape(ROWS * 6, turns, 8, VCAP), *masks)


def contract(turns, w_rows, t_rows, *masks):
    partial = product(turns, w_rows, t_rows)
    by_z = lax.psum_scatter(partial, "z", scatter_dimension=0, tiled=True)
    out = send_out(by_z.reshape(4, BLOCK, turns * VCAP), *masks)
    return lax.all_to_all(out, ("y", "core", "x"), 0, 0, tiled=True)


def per_device(w_cycle, amplitudes, occ_count, virt_count, target):
    row = lax.axis_index("y") * 2 + lax.axis_index("core")
    col = lax.axis_index("x") * 8 + lax.axis_index("z")
    masks = (jnp.stack([row, col]).astype(jnp.int32), occ_count, virt_count, target)
    *dealt, which = deal(amplitudes, occ_count, virt_count, target)
    w_rows = lax.all_gather(w_cycle, ("y", "core"), axis=0, tiled=True)
    t_rows = lax.switch(
        which[0], [functools.partial(bring, turns) for turns in SIZES], dealt, *masks
    )
    got = lax.switch(
        which[0], [functools.partial(contract, turns) for turns in SIZES], w_rows, t_rows, *masks
    )
    return place(got, *masks)


def solution(mesh):
    chips = Mesh(mesh.devices.reshape(8, 2, 4, 8), ("y", "core", "x", "z"))
    row, col = ("y", "core"), ("x", "z")
    placed = (P(row, col), P(col, None, row, None), P(), P(), P())
    return jax.shard_map(
        per_device, mesh=chips, in_specs=placed, out_specs=P(col, row), check_vma=False
    )
```
